32 devices in a mesh: chan: 16 (over z, x, core), tm: 2 (over y).
Axes of the slice: x: 2, y: 2, z: 4, core: 2. Of those that a mesh axis runs over, the one named last changes fastest.
Arguments:
- raw_strain: bfloat16 [2048, 16384], P('chan', 'tm'), may hold values from -6 to 6
- fir_taps: bfloat16 [64], replicated, may hold values from -0.75 to 0.75
- sources: int32 [2, 8], replicated, may hold values from 0 to 2047, as said below
Outputs:
- correlation: float32 [2, 8, 257, 2048], P(None, 'tm', None, 'chan')
The draws below stay inside these ranges and needn't reach their ends.
Inputs may be any that keep to these rules, and one draw needn't show every extreme that they name: `sources`: the 16 entries are distinct channel indices; the first and the last channel are always among them.
All inputs are finite; a program needn't handle non-finite values.
Results may differ from the reference program's by a relative error of at most 0.0037.
Values may be sent and summed in bfloat16 or wider, within the bound.
A program may use at most 64 MiB of HBM per device.

```python
import math
import jax
import jax.numpy as jnp
from jax import lax

CH_DEV = 128
TAPS = 64
DECIM = 4
HALF_WIN = 32
LAGS = 257
HALF_LAG = 128
STEPS = 2
PER_STEP = 8
SOURCES = 16
CHANNELS = 2048
DEC = 4096
RAW = 16384
N_CHAN = 16


def draw_sources(key, part):
    first_key = jax.random.fold_in(key, 11)
    second_key = jax.random.fold_in(key, 23)
    middle = jax.random.permutation(first_key, CHANNELS - 2)[:STEPS * PER_STEP - 2] + 1
    ends = jnp.array([0, CHANNELS - 1], jnp.int32)
    entries = jnp.concatenate([ends, middle.astype(jnp.int32)])
    order = jax.random.permutation(second_key, STEPS * PER_STEP)
    return entries[order].reshape(STEPS, PER_STEP).astype(jnp.int32)


def block_levels(own_key, extent, split, least, largest):
    loudness, own = 1.0, jax.random.fold_in(own_key, 6)
    for axis_at, blocks in split:
        draws = jnp.exp(jax.random.uniform(jax.random.fold_in(own, axis_at), (blocks,), jnp.float32, least / len(split), largest / len(split)))
        loudness = loudness * jnp.repeat(draws, extent[axis_at] // blocks).reshape([-1 if axis == axis_at else 1 for axis in range(len(extent))])
    return loudness


def normal_values(own_key, extent, width, limit, shards=(), held_as=jnp.bfloat16):
    factor_of = block_levels(own_key, extent, shards, -0.22, 0.18) if shards else 1.0
    values = jax.random.normal(own_key, extent, jnp.float32) * width * factor_of
    return jnp.minimum(jnp.maximum(values, -limit), limit).astype(held_as)


def setup_inputs(seed: int = 0) -> dict:
    streams_of = jax.random.split(jax.random.key(seed), 4)
    raw_strain = normal_values(streams_of[0], (CHANNELS, RAW), 1.0, 6.0, ((0, 16), (1, 2)))
    fir_taps = normal_values(streams_of[1], (TAPS,), TAPS ** -0.5, 0.75)
    sources = draw_sources(jax.random.fold_in(streams_of[3], 71), 0)
    return dict(raw_strain=raw_strain, fir_taps=fir_taps, sources=sources)


def reference(raw_strain, fir_taps, sources):
    taps_wide = fir_taps.astype(jnp.float32)

    def clean(block):
        padded = jnp.pad(block.astype(jnp.float32), ((0, 0), (TAPS, 0)))
        decimated = jnp.zeros((block.shape[0], DEC), jnp.float32)
        for tap_index in range(TAPS):
            begin = TAPS - tap_index
            decimated = decimated + taps_wide[tap_index] * padded[:, begin:begin + DECIM * DEC:DECIM]
        magnitude = jnp.pad(jnp.abs(decimated), ((0, 0), (HALF_WIN, HALF_WIN)))
        window_total = jnp.zeros((block.shape[0], DEC), jnp.float32)
        for offset in range(2 * HALF_WIN + 1):
            window_total = window_total + magnitude[:, offset:offset + DEC]
        level = window_total / (2 * HALF_WIN + 1) + 1e-05
        return (decimated / level).astype(jnp.bfloat16)
    white = lax.map(clean, raw_strain.reshape(N_CHAN, CH_DEV, RAW)).reshape(CHANNELS, DEC)
    traces = white[sources.reshape(-1).astype(jnp.int32)].astype(jnp.float32)
    length = DEC + LAGS - 1
    trace_spectra = jnp.conj(jnp.fft.rfft(traces, n=length, axis=-1))

    def correlate(block):
        spectra = jnp.fft.rfft(block.astype(jnp.float32), n=length, axis=-1)
        circular = jnp.fft.irfft(trace_spectra[:, None, :] * spectra[None, :, :], n=length, axis=-1)
        lagged = jnp.concatenate([circular[..., length - HALF_LAG:], circular[..., :HALF_LAG + 1]], axis=-1)
        return jnp.transpose(lagged, (0, 2, 1))
    blocks = lax.map(correlate, white.reshape(N_CHAN, CH_DEV, DEC))
    result = jnp.transpose(blocks, (1, 2, 0, 3)).reshape(SOURCES, LAGS, CHANNELS)
    result = result / math.sqrt(DEC)
    return result.reshape(STEPS, PER_STEP, LAGS, CHANNELS).astype(jnp.float32)
```

```python
import functools
import math

import jax
import jax.numpy as jnp
from jax import lax
from jax.experimental import pallas as pl
from jax.experimental.pallas import tpu as pltpu
from jax.sharding import PartitionSpec as P

TAPS = 64
DECIM = 4
HALF_WIN = 32
LAGS = 257
HALF_LAG = 128
STEPS = 2
W = 128
SLAB = 8
EARLY = 3
BLOCK = 1024
LEFT = 256
RIGHT = 128
MESH = pl.DeviceIdType.MESH


def nt(a, b):
    return lax.dot_general(
        a, b, (((1,), (1,)), ((), ())), preferred_element_type=jnp.float32
    )


def aligned(x):
    return pl.multiple_of(x, W)


def kernel(
    C, T, scale,
    raw_ref, taps_hbm, src_hbm, out_ref,
    taps_ref, src_ref, x_ref, dec_ref, hi_ref, lo_ref, white_ref, send1, recv1, recv2, rep_ref, shifted, acc_ref,
    small_sem, load_sem, halo_send, halo_recv, s1_sem, r1_sem, s2_sem, r2_sem, bulk_send, bulk_recv,
):
    c = lax.axis_index("chan")
    t = lax.axis_index("tm")
    N = C * T
    rows, raw_len = raw_ref.shape
    dec_len = raw_len // DECIM
    nb = dec_len // W
    half = nb // ((T * nb) // C)
    step_len = src_hbm.shape[1] // T
    ns = STEPS * step_len
    me = c * T + t
    total = T * dec_len
    mine = t * dec_len

    barrier = pltpu.get_barrier_semaphore()

    def greet(d, _):
        other = lax.rem(me + d, N)
        pl.semaphore_signal(
            barrier, inc=1, device_id=(other // T, lax.rem(other, T)), device_id_type=MESH
        )
        return 0

    lax.fori_loop(1, N, greet, 0)

    small = [
        pltpu.make_async_copy(taps_hbm, taps_ref, small_sem.at[0]),
        pltpu.make_async_copy(src_hbm, src_ref, small_sem.at[1]),
    ]
    for copy in small:
        copy.start()
    seg = raw_len // half
    loads = []
    for i in range(half):
        load = pltpu.make_async_copy(
            raw_ref.at[:, pl.ds(i * seg, seg)],
            x_ref.at[:, pl.ds(LEFT + i * seg, seg)],
            load_sem.at[i],
        )
        load.start()
        loads.append(load)

    span = lax.broadcasted_iota(jnp.int32, (2 * W, 4 * W), 1) - W - lax.broadcasted_iota(
        jnp.int32, (2 * W, 4 * W), 0
    )
    band = jnp.where((span >= -HALF_WIN) & (span <= HALF_WIN), 1.0, 0.0).astype(jnp.bfloat16)

    for copy in small:
        copy.wait()

    taps = jnp.broadcast_to(taps_ref[...], (16, TAPS))
    place = lax.broadcasted_iota(jnp.int32, (TAPS, W), 1) == lax.rem(
        W - lax.broadcasted_iota(jnp.int32, (TAPS, W), 0), W
    )
    base = jnp.dot(
        taps, place.astype(jnp.float32).astype(jnp.bfloat16), preferred_element_type=jnp.float32
    )
    rolled = pltpu.roll(
        jnp.broadcast_to(base[0:1, :], (W, W)), 0, 1, stride=DECIM, stride_axis=0
    )
    row_id = lax.broadcasted_iota(jnp.int32, (W, W), 0)
    lane_id = lax.broadcasted_iota(jnp.int32, (W, W), 1)
    fts = []
    for jc in range(DECIM + 1):
        k = DECIM * row_id + W - W * jc - lane_id
        fts.append(jnp.where((k >= 0) & (k < W), rolled, 0.0).astype(jnp.bfloat16))
    ft = jnp.concatenate(fts, axis=1)

    pr = lax.broadcasted_iota(jnp.int32, (T * SLAB, rows), 0)
    pc = lax.broadcasted_iota(jnp.int32, (T * SLAB, rows), 1)
    picks = jnp.zeros((T * SLAB, rows), jnp.float32)
    for g in range(T):
        for step in range(STEPS):
            for p in range(step_len):
                local = src_ref[step, g * step_len + p] - c * rows
                hit = (pr == g * SLAB + step * step_len + p) & (pc == local)
                picks = jnp.where(hit, 1.0, picks)
    picks = picks.astype(jnp.bfloat16)

    to_right = pltpu.make_async_remote_copy(
        src_ref=raw_ref.at[:, pl.ds(raw_len - LEFT, LEFT)],
        dst_ref=x_ref.at[:, pl.ds(0, LEFT)],
        send_sem=halo_send.at[0], recv_sem=halo_recv.at[0],
        device_id=(c, lax.rem(t + 1, T)), device_id_type=MESH,
    )
    to_left = pltpu.make_async_remote_copy(
        src_ref=raw_ref.at[:, pl.ds(0, RIGHT)],
        dst_ref=x_ref.at[:, pl.ds(LEFT + raw_len, RIGHT)],
        send_sem=halo_send.at[1], recv_sem=halo_recv.at[1],
        device_id=(c, lax.rem(t + T - 1, T)), device_id_type=MESH,
    )

    def put_mag(b, d):
        mag = jnp.abs(d)
        hi = mag.astype(jnp.bfloat16)
        hi_ref[:, (b + 1) * W:(b + 2) * W] = hi
        lo_ref[:, (b + 1) * W:(b + 2) * W] = (mag - hi.astype(jnp.float32)).astype(jnp.bfloat16)

    def chunk(b):
        begin = LEFT - W + b * DECIM * W
        d = nt(x_ref[:, begin:begin + (DECIM + 1) * W], ft)
        dec_ref[:, b * W:(b + 1) * W] = d
        put_mag(b, d)

    def first(g, i):
        k = g * half + i
        dest = t * half + i
        self_hit = (dest == c) & (g == t)
        remote = pltpu.make_async_remote_copy(
            src_ref=send1.at[k], dst_ref=recv1.at[c],
            send_sem=s1_sem.at[k], recv_sem=r1_sem,
            device_id=(dest, g), device_id_type=MESH,
        )
        return self_hit, remote

    def start_first(g, i):
        self_hit, remote = first(g, i)

        @pl.when(jnp.logical_not(self_hit))
        def _():
            remote.start()

        @pl.when(self_hit)
        def _():
            pltpu.make_async_copy(send1.at[g * half + i], recv1.at[c], r1_sem).start()

    def end_first(g, i):
        self_hit, remote = first(g, i)

        @pl.when(jnp.logical_not(self_hit))
        def _():
            remote.wait_send()

    def bulk(d, i):
        cols = pl.ds(aligned(mine + i * 2 * W), 2 * W)
        return pltpu.make_async_remote_copy(
            src_ref=white_ref.at[:, cols], dst_ref=white_ref.at[:, cols],
            send_sem=bulk_send.at[d - 1, i], recv_sem=bulk_recv.at[d - 1, i],
            device_id=(c, lax.rem(t + d, T)), device_id_type=MESH,
        )

    def pair(p):
        cols = slice(2 * p * W, (2 * p + 4) * W)
        sums = nt(hi_ref[:, cols], band) + nt(lo_ref[:, cols], band)
        level = sums / (2 * HALF_WIN + 1) + 1e-05
        w = (dec_ref[:, 2 * p * W:2 * (p + 1) * W] / level).astype(jnp.bfloat16)
        white_ref[:, pl.ds(aligned(mine + 2 * p * W), 2 * W)] = w
        picked = jnp.dot(picks, w, preferred_element_type=jnp.float32)
        for g in range(T):
            send1[g * half + p] = jnp.concatenate(
                [picked[g * SLAB:(g + 1) * SLAB, h * W:(h + 1) * W] for h in range(2)], axis=0
            ).astype(jnp.bfloat16)

    def all_bulk(i):
        for d in range(1, T):
            bulk(d, i).start()

    order = list(range(1, half - 1)) + [0, half - 1]
    done = {0}
    here = 0
    for at, p in enumerate(order):
        if p == 0:
            @pl.when(t > 0)
            def _():
                to_right.wait_recv()

            @pl.when(t < T - 1)
            def _():
                to_left.wait_recv()

            chunk(0)
            before = nt(x_ref[:, 0:LEFT], ft[:, 3 * W:5 * W])
            keep = (t > 0) & (lax.broadcasted_iota(jnp.int32, (rows, W), 1) >= W - HALF_WIN)
            put_mag(-1, jnp.where(keep, before, 0.0))
            after = nt(x_ref[:, LEFT + raw_len - W:LEFT + raw_len + RIGHT], ft[:, 0:2 * W])
            keep = (t < T - 1) & (lax.broadcasted_iota(jnp.int32, (rows, W), 1) < HALF_WIN)
            put_mag(nb, jnp.where(keep, after, 0.0))
        for b in range(2 * p - 1, min(2 * p + 3, nb)):
            if b >= 0 and b not in done:
                while here <= b // 2:
                    loads[here].wait()
                    here += 1
                chunk(b)
                done.add(b)
        pair(p)
        if at == 0:
            pl.semaphore_wait(barrier, N - 1)

            @pl.when(t < T - 1)
            def _():
                to_right.start()

            @pl.when(t > 0)
            def _():
                to_left.start()

            @pl.when(t == 0)
            def _():
                x_ref[:, 0:LEFT] = jnp.zeros((rows, LEFT), jnp.bfloat16)

            @pl.when(t == T - 1)
            def _():
                x_ref[:, LEFT + raw_len:] = jnp.zeros((rows, RIGHT), jnp.bfloat16)

        for g in range(T):
            start_first(g, p)
        if at < EARLY:
            all_bulk(p)

    shifted[0:W, :] = jnp.zeros((W, W), jnp.bfloat16)

    def each(count, body):
        if count <= 16:
            for i in range(count):
                body(i)
            return

        def step(i, _):
            body(i)
            return 0

        lax.fori_loop(0, count, step, 0)

    pltpu.make_async_copy(recv1, recv1, r1_sem).wait()
    summed = recv1[0].astype(jnp.float32)
    for j in range(1, C):
        summed = summed + recv1[j].astype(jnp.float32)
    send1[T * half] = summed.astype(jnp.bfloat16)

    def second(d):
        return pltpu.make_async_remote_copy(
            src_ref=send1.at[T * half], dst_ref=recv2.at[c],
            send_sem=s2_sem.at[d], recv_sem=r2_sem,
            device_id=(lax.rem(c + d + 1, C), t), device_id_type=MESH,
        )

    each(C - 1, lambda d: second(d).start())
    pltpu.make_async_copy(send1.at[T * half], recv2.at[c], r2_sem).start()
    for i in order[EARLY:]:
        all_bulk(i)
    pltpu.make_async_copy(recv2, recv2, r2_sem).wait()

    lags = W // ns
    tall = lags * step_len
    tiles = tall // SLAB
    group = SLAB // step_len
    gathered = jnp.concatenate([recv2[j] for j in range(C)], axis=1)
    spread_row = lax.broadcasted_iota(jnp.int32, (2 * STEPS * SLAB, 2 * SLAB), 0)
    spread_col = lax.broadcasted_iota(jnp.int32, (2 * STEPS * SLAB, 2 * SLAB), 1)
    wanted = (spread_row // (STEPS * SLAB)) * SLAB + (spread_row // SLAB % STEPS) * step_len + (
        spread_row % step_len
    )
    spread = jnp.where(spread_col == wanted, 1.0, 0.0).astype(jnp.bfloat16)
    rep_ref[...] = jnp.dot(spread, gathered, preferred_element_type=jnp.float32)
    low = lax.broadcasted_iota(jnp.int32, (SLAB, W), 0) // step_len
    low_lane = lax.broadcasted_iota(jnp.int32, (SLAB, W), 1) - low
    zero = jnp.zeros((SLAB, W), jnp.float32)

    def build(j, prev):
        for h in range(2):
            now = []
            for step in range(STEPS):
                top = (h * STEPS + step) * SLAB
                x = rep_ref[top:top + SLAB, pl.ds(aligned(j * W), W)]
                start = x
                for k in range(1, group):
                    start = jnp.where(low == k, pltpu.roll(x, k, 1), start)
                for v in range(tiles):
                    now.append(pltpu.roll(start, v * group, 1) if v else start)
            put_shifted(aligned((2 * j + h + 1) * W), now, prev)
            prev = tuple(now)
        return prev

    def put_shifted(at, now, prev):
        z = jnp.concatenate(
            [
                jnp.where(low_lane >= (v % tiles) * group, now[v], prev[v])
                for v in range(STEPS * tiles)
            ],
            axis=0,
        )
        shifted[pl.ds(at, W), :] = z.T.astype(jnp.bfloat16)

    last = lax.fori_loop(0, C, build, (zero,) * (STEPS * tiles))
    put_shifted(W + total, (zero,) * (STEPS * tiles), last)

    groups = 2 * HALF_LAG // lags + 1

    def products(n, count, fresh=False):
        w = white_ref[:, pl.ds(aligned(n), count)]
        for k in range(0, groups, 2):
            b = jnp.concatenate(
                [
                    shifted[pl.ds(pl.multiple_of(n + 2 * HALF_LAG - lags * m, 16), count), :]
                    for m in range(k, min(k + 2, groups))
                ],
                axis=1,
            )
            out = jnp.dot(w, b, preferred_element_type=jnp.float32)
            cols = slice(k * W, k * W + b.shape[1])
            if fresh:
                acc_ref[:, cols] = out
            else:
                acc_ref[:, cols] += out

    block = min(BLOCK, dec_len)
    for q in range(dec_len // block):
        products(mine + q * block, block, q == 0)

    def arrive(d, i):
        at = lax.rem(t + T - d, T) * dec_len + i * 2 * W
        cols = pl.ds(aligned(at), 2 * W)
        pltpu.make_async_copy(
            white_ref.at[:, cols], white_ref.at[:, cols], bulk_recv.at[d - 1, i]
        ).wait()
        products(at, 2 * W)

    def arrivals(d, _):
        for i in order:
            arrive(d, i)
        return 0

    if T == 2:
        arrivals(1, 0)
    else:
        lax.fori_loop(1, T, arrivals, 0)

    for k in range(groups):
        block = acc_ref[:, k * W:(k + 1) * W].T * scale
        for step in range(STEPS):
            to = (step * LAGS + k * lags) * step_len
            size = tall if k < groups - 1 else step_len
            out_ref[to:to + size, :] = block[step * tall:step * tall + size, :]

    @pl.when(t < T - 1)
    def _():
        to_right.wait_send()

    @pl.when(t > 0)
    def _():
        to_left.wait_send()

    for g in range(T):
        each(half, lambda i: end_first(g, i))
    each(C - 1, lambda d: second(d).wait_send())
    for d in range(1, T):
        for i in range(half):
            bulk(d, i).wait_send()


def per_device(C, T, raw_strain, fir_taps, sources):
    rows, raw_len = raw_strain.shape
    dec_len = raw_len // DECIM
    nb = dec_len // W
    half = nb * C // (T * nb)
    step_len = sources.shape[1] // T
    ns = STEPS * step_len
    total = T * dec_len
    groups = 2 * HALF_LAG // (W // ns) + 1
    bf, f32 = jnp.bfloat16, jnp.float32
    flat = pl.pallas_call(
        functools.partial(kernel, C, T, 1.0 / math.sqrt(total)),
        out_shape=pltpu.VMEM((STEPS * LAGS * step_len, rows), f32),
        in_specs=[
            pl.BlockSpec(memory_space=pltpu.HBM),
            pl.BlockSpec(memory_space=pltpu.HBM),
            pl.BlockSpec(memory_space=pltpu.HBM),
        ],
        out_specs=pl.BlockSpec(memory_space=pltpu.VMEM),
        scratch_shapes=[
            pltpu.VMEM((1, TAPS), bf),
            pltpu.SMEM(sources.shape, jnp.int32),
            pltpu.VMEM((rows, LEFT + raw_len + RIGHT), bf),
            pltpu.VMEM((rows, dec_len), f32),
            pltpu.VMEM((rows, dec_len + 2 * W), bf),
            pltpu.VMEM((rows, dec_len + 2 * W), bf),
            pltpu.VMEM((rows, total), bf),
            pltpu.VMEM((T * half + 1, 16, W), bf),
            pltpu.VMEM((C, 16, W), bf),
            pltpu.VMEM((C, 16, W), bf),
            pltpu.VMEM((2 * STEPS * SLAB, C * W), f32),
            pltpu.VMEM((total + 2 * W, W), bf),
            pltpu.VMEM((rows, groups * W), f32),
            pltpu.SemaphoreType.DMA((2,)),
            pltpu.SemaphoreType.DMA((half,)),
            pltpu.SemaphoreType.DMA((2,)),
            pltpu.SemaphoreType.DMA((2,)),
            pltpu.SemaphoreType.DMA((T * half,)),
            pltpu.SemaphoreType.DMA,
            pltpu.SemaphoreType.DMA((C,)),
            pltpu.SemaphoreType.DMA,
            pltpu.SemaphoreType.DMA((T, half)),
            pltpu.SemaphoreType.DMA((T, half)),
        ],
        compiler_params=pltpu.CompilerParams(
            collective_id=0, has_side_effects=True, vmem_limit_bytes=62 * 1024 * 1024
        ),
    )(raw_strain, fir_taps.reshape(1, TAPS), sources)
    return jnp.swapaxes(flat.reshape(STEPS, LAGS, step_len, rows), 1, 2)


def solution(mesh):
    C, T = mesh.shape["chan"], mesh.shape["tm"]
    return jax.shard_map(
        functools.partial(per_device, C, T),
        mesh=mesh,
        in_specs=(P("chan", "tm"), P(), P()),
        out_specs=P(None, "tm", None, "chan"),
        check_vma=False,
    )
```

```python
import functools
import math

import jax
import jax.numpy as jnp
from jax import lax
from jax.experimental import pallas as pl
from jax.experimental.pallas import tpu as pltpu
from jax.sharding import PartitionSpec as P

TAPS = 64
DECIM = 4
HALF_WIN = 32
LAGS = 257
HALF_LAG = 128
STEPS = 2
W = 128
SLAB = 8
LEAD = 1
FIRST = 2
EARLY = 4
BLOCK = 1024
LEFT = 256
RIGHT = 128
MESH = pl.DeviceIdType.MESH


def nt(a, b):
    return lax.dot_general(
        a, b, (((1,), (1,)), ((), ())), preferred_element_type=jnp.float32
    )


def aligned(x):
    return pl.multiple_of(x, W)


def kernel(
    C, T, scale,
    raw_ref, taps_hbm, src_hbm, out_ref,
    taps_ref, src_ref, x_ref, dec_ref, hi_ref, lo_ref, white_ref, send1, recv1, recv2, window_ref, shift_ref, shifted, acc_ref,
    small_sem, load_sem, halo_send, halo_recv, s1_sem, r1_sem, s2_sem, r2_sem, bulk_send, bulk_recv,
):
    c = lax.axis_index("chan")
    t = lax.axis_index("tm")
    N = C * T
    rows, raw_len = raw_ref.shape
    dec_len = raw_len // DECIM
    nb = dec_len // W
    half = nb // ((T * nb) // C)
    step_len = src_hbm.shape[1] // T
    ns = STEPS * step_len
    me = c * T + t
    total = T * dec_len
    mine = t * dec_len

    barrier = pltpu.get_barrier_semaphore()

    def greet(d, _):
        other = lax.rem(me + d, N)
        pl.semaphore_signal(
            barrier, inc=1, device_id=(other // T, lax.rem(other, T)), device_id_type=MESH
        )
        return 0

    lax.fori_loop(1, N, greet, 0)

    small = [
        pltpu.make_async_copy(taps_hbm, taps_ref, small_sem.at[0]),
        pltpu.make_async_copy(src_hbm, src_ref, small_sem.at[1]),
    ]
    for copy in small:
        copy.start()
    seg = raw_len // half
    loads = []
    for i in range(half):
        load = pltpu.make_async_copy(
            raw_ref.at[:, pl.ds(i * seg, seg)],
            x_ref.at[:, pl.ds(LEFT + i * seg, seg)],
            load_sem.at[i],
        )
        load.start()
        loads.append(load)

    span = lax.broadcasted_iota(jnp.int32, (2 * W, 4 * W), 1) - W - lax.broadcasted_iota(
        jnp.int32, (2 * W, 4 * W), 0
    )
    band = jnp.where((span >= -HALF_WIN) & (span <= HALF_WIN), 1.0, 0.0).astype(jnp.bfloat16)

    for copy in small:
        copy.wait()

    taps = jnp.broadcast_to(taps_ref[...], (16, TAPS))
    place = lax.broadcasted_iota(jnp.int32, (TAPS, W), 1) == lax.rem(
        W - lax.broadcasted_iota(jnp.int32, (TAPS, W), 0), W
    )
    base = jnp.dot(
        taps, place.astype(jnp.float32).astype(jnp.bfloat16), preferred_element_type=jnp.float32
    )
    rolled = pltpu.roll(
        jnp.broadcast_to(base[0:1, :], (W, W)), 0, 1, stride=DECIM, stride_axis=0
    )
    row_id = lax.broadcasted_iota(jnp.int32, (W, W), 0)
    lane_id = lax.broadcasted_iota(jnp.int32, (W, W), 1)
    fts = []
    for jc in range(DECIM + 1):
        k = DECIM * row_id + W - W * jc - lane_id
        fts.append(jnp.where((k >= 0) & (k < W), rolled, 0.0).astype(jnp.bfloat16))
    ft = jnp.concatenate(fts, axis=1)

    pr = lax.broadcasted_iota(jnp.int32, (T * SLAB, rows), 0)
    pc = lax.broadcasted_iota(jnp.int32, (T * SLAB, rows), 1)
    picks = jnp.zeros((T * SLAB, rows), jnp.float32)
    for g in range(T):
        for step in range(STEPS):
            for p in range(step_len):
                local = src_ref[step, g * step_len + p] - c * rows
                hit = (pr == g * SLAB + step * step_len + p) & (pc == local)
                picks = jnp.where(hit, 1.0, picks)
    picks = picks.astype(jnp.bfloat16)

    to_right = pltpu.make_async_remote_copy(
        src_ref=raw_ref.at[:, pl.ds(raw_len - LEFT, LEFT)],
        dst_ref=x_ref.at[:, pl.ds(0, LEFT)],
        send_sem=halo_send.at[0], recv_sem=halo_recv.at[0],
        device_id=(c, lax.rem(t + 1, T)), device_id_type=MESH,
    )
    to_left = pltpu.make_async_remote_copy(
        src_ref=raw_ref.at[:, pl.ds(0, RIGHT)],
        dst_ref=x_ref.at[:, pl.ds(LEFT + raw_len, RIGHT)],
        send_sem=halo_send.at[1], recv_sem=halo_recv.at[1],
        device_id=(c, lax.rem(t + T - 1, T)), device_id_type=MESH,
    )

    def put_mag(b, d):
        mag = jnp.abs(d)
        hi = mag.astype(jnp.bfloat16)
        hi_ref[:, (b + 1) * W:(b + 2) * W] = hi
        lo_ref[:, (b + 1) * W:(b + 2) * W] = (mag - hi.astype(jnp.float32)).astype(jnp.bfloat16)

    def decimate(blocks):
        begins = [LEFT - W + b * DECIM * W for b in blocks]
        x = jnp.concatenate([x_ref[:, a:a + (DECIM + 1) * W] for a in begins], axis=0)
        d = nt(x, ft)
        for i, b in enumerate(blocks):
            mine_d = d[i * rows:(i + 1) * rows]
            dec_ref[:, b * W:(b + 1) * W] = mine_d
            put_mag(b, mine_d)

    def first(g, i):
        k = g * half + i
        dest = i * T + t
        self_hit = (dest == c) & (g == t)
        remote = pltpu.make_async_remote_copy(
            src_ref=send1.at[k], dst_ref=recv1.at[c],
            send_sem=s1_sem.at[k], recv_sem=r1_sem,
            device_id=(dest, g), device_id_type=MESH,
        )
        return self_hit, remote

    def start_first(g, i):
        self_hit, remote = first(g, i)

        @pl.when(jnp.logical_not(self_hit))
        def _():
            remote.start()

        @pl.when(self_hit)
        def _():
            pltpu.make_async_copy(send1.at[g * half + i], recv1.at[c], r1_sem).start()

    def end_first(g, i):
        self_hit, remote = first(g, i)

        @pl.when(jnp.logical_not(self_hit))
        def _():
            remote.wait_send()

    def bulk(d, i):
        cols = pl.ds(aligned(mine + i * 2 * W), 2 * W)
        return pltpu.make_async_remote_copy(
            src_ref=white_ref.at[:, cols], dst_ref=white_ref.at[:, cols],
            send_sem=bulk_send.at[d - 1, i], recv_sem=bulk_recv.at[d - 1, i],
            device_id=(c, lax.rem(t + d, T)), device_id_type=MESH,
        )

    def whiten(pairs):
        cols = [slice(2 * p * W, (2 * p + 4) * W) for p in pairs]
        sums = nt(jnp.concatenate([hi_ref[:, q] for q in cols], axis=0), band) + nt(
            jnp.concatenate([lo_ref[:, q] for q in cols], axis=0), band
        )
        level = sums / (2 * HALF_WIN + 1) + 1e-05
        for i, p in enumerate(pairs):
            d = dec_ref[:, 2 * p * W:2 * (p + 1) * W]
            w = (d / level[i * rows:(i + 1) * rows]).astype(jnp.bfloat16)
            white_ref[:, pl.ds(aligned(mine + 2 * p * W), 2 * W)] = w
            picked = jnp.dot(picks, w, preferred_element_type=jnp.float32)
            for g in range(T):
                send1[g * half + p] = jnp.concatenate(
                    [picked[g * SLAB:(g + 1) * SLAB, h * W:(h + 1) * W] for h in range(2)],
                    axis=0,
                ).astype(jnp.bfloat16)

    def all_bulk(i):
        for d in range(1, T):
            bulk(d, i).start()

    def spread_out(pairs):
        for p in pairs:
            for g in range(T):
                start_first(g, p)

    order = list(range(1, half - 1)) + [0, half - 1]
    lead = order[:LEAD]
    inner = order[LEAD:half - 2]
    edge = order[half - 2:]

    pl.semaphore_wait(barrier, N - 1)

    @pl.when(t < T - 1)
    def _():
        to_right.start()

    @pl.when(t > 0)
    def _():
        to_left.start()

    @pl.when(t == 0)
    def _():
        x_ref[:, 0:LEFT] = jnp.zeros((rows, LEFT), jnp.bfloat16)

    @pl.when(t == T - 1)
    def _():
        x_ref[:, LEFT + raw_len:] = jnp.zeros((rows, RIGHT), jnp.bfloat16)

    split = 2 * LEAD + 3
    for i in range(-(-split // 2)):
        loads[i].wait()
    decimate(range(1, split))
    whiten(lead)
    spread_out(lead)
    for p in lead:
        all_bulk(p)
    for i in range(-(-split // 2), half):
        loads[i].wait()
    decimate(range(split, nb))
    whiten(inner)
    spread_out(inner)
    for p in order[LEAD:FIRST]:
        all_bulk(p)

    @pl.when(t > 0)
    def _():
        to_right.wait_recv()

    @pl.when(t < T - 1)
    def _():
        to_left.wait_recv()

    decimate([0])
    past = nt(x_ref[:, 0:LEFT], ft[:, 3 * W:5 * W])
    keep = (t > 0) & (lax.broadcasted_iota(jnp.int32, (rows, W), 1) >= W - HALF_WIN)
    put_mag(-1, jnp.where(keep, past, 0.0))
    after = nt(x_ref[:, LEFT + raw_len - W:LEFT + raw_len + RIGHT], ft[:, 0:2 * W])
    keep = (t < T - 1) & (lax.broadcasted_iota(jnp.int32, (rows, W), 1) < HALF_WIN)
    put_mag(nb, jnp.where(keep, after, 0.0))
    whiten(edge)
    spread_out(edge)
    for p in order[FIRST:EARLY]:
        all_bulk(p)

    shifted[0:W, :] = jnp.zeros((W, W), jnp.bfloat16)
    lags = W // ns
    tall = lags * step_len
    tiles = tall // SLAB
    group = SLAB // step_len
    sample = lax.broadcasted_iota(jnp.int32, (2 * W, tiles * W), 0)
    place = lax.broadcasted_iota(jnp.int32, (2 * W, tiles * W), 1)
    shift = jnp.where(sample == W + place % W - place // W * group, 1.0, 0.0)
    shift_ref[...] = shift.astype(jnp.bfloat16)

    def each(count, body):
        if count <= 16:
            for i in range(count):
                body(i)
            return

        def step(i, _):
            body(i)
            return 0

        lax.fori_loop(0, count, step, 0)

    pltpu.make_async_copy(recv1, recv1, r1_sem).wait()
    summed = recv1[0].astype(jnp.float32)
    for j in range(1, C):
        summed = summed + recv1[j].astype(jnp.float32)
    send1[T * half] = summed.astype(jnp.bfloat16)

    def second(d):
        return pltpu.make_async_remote_copy(
            src_ref=send1.at[T * half], dst_ref=recv2.at[c],
            send_sem=s2_sem.at[d], recv_sem=r2_sem,
            device_id=(lax.rem(c + d + 1, C), t), device_id_type=MESH,
        )

    each(C - 1, lambda d: second(d).start())
    pltpu.make_async_copy(send1.at[T * half], recv2.at[c], r2_sem).start()
    for i in order[EARLY:]:
        all_bulk(i)
    pltpu.make_async_copy(recv2, recv2, r2_sem).wait()

    gathered = jnp.concatenate([recv2[q % half * T + q // half] for q in range(C)], axis=1)
    spread_row = lax.broadcasted_iota(jnp.int32, (2 * STEPS * SLAB, 2 * SLAB), 0)
    spread_col = lax.broadcasted_iota(jnp.int32, (2 * STEPS * SLAB, 2 * SLAB), 1)
    wanted = (spread_row // (STEPS * SLAB)) * SLAB + (spread_row // SLAB % STEPS) * step_len + (
        spread_row % step_len
    )
    spread = jnp.where(spread_col == wanted, 1.0, 0.0).astype(jnp.bfloat16)
    rep = jnp.dot(spread, gathered, preferred_element_type=jnp.float32)
    low = lax.broadcasted_iota(jnp.int32, (SLAB, W), 0) // step_len
    lane = lax.broadcasted_iota(jnp.int32, (SLAB, W), 1)
    zero = jnp.zeros((SLAB, W), jnp.float32)
    before = [zero] * STEPS
    turned = [[zero] * group] * STEPS
    for q in range(2 * C + 1):
        for step in range(STEPS):
            if q < 2 * C:
                top = (q % 2 * STEPS + step) * SLAB
                x = rep[top:top + SLAB, q // 2 * W:(q // 2 + 1) * W]
                turn = [x] + [pltpu.roll(x, k, 1) for k in range(1, group)]
            else:
                x, turn = zero, [zero] * group
            for k in range(1, group):
                x = jnp.where(
                    low == k, jnp.where(lane >= k, turn[k], turned[step][k]), x
                )
            turned = turned[:step] + [turn] + turned[step + 1:]
            at = (q * STEPS + step) * SLAB
            window_ref[at:at + SLAB, 0:W] = before[step]
            window_ref[at:at + SLAB, W:] = x
            before[step] = x
    batch = 12
    for q in range(0, 2 * C + 1, batch):
        count = min(batch, 2 * C + 1 - q)
        span = STEPS * SLAB
        moved = jnp.dot(
            window_ref[q * span:(q + count) * span, :].astype(jnp.bfloat16), shift_ref[...],
            preferred_element_type=jnp.float32,
        )
        for i in range(count):
            z = jnp.concatenate(
                [
                    moved[(i * STEPS + step) * SLAB:(i * STEPS + step + 1) * SLAB, v * W:(v + 1) * W]
                    for step in range(STEPS)
                    for v in range(tiles)
                ],
                axis=0,
            )
            shifted[(q + i + 1) * W:(q + i + 2) * W, :] = z.T.astype(jnp.bfloat16)

    groups = 2 * HALF_LAG // lags + 1

    def products(n, count, fresh=False):
        w = white_ref[:, pl.ds(aligned(n), count)]
        for k in range(0, groups, 2):
            b = jnp.concatenate(
                [
                    shifted[pl.ds(pl.multiple_of(n + 2 * HALF_LAG - lags * m, 16), count), :]
                    for m in range(k, min(k + 2, groups))
                ],
                axis=1,
            )
            out = jnp.dot(w, b, preferred_element_type=jnp.float32)
            cols = slice(k * W, k * W + b.shape[1])
            if fresh:
                acc_ref[:, cols] = out
            else:
                acc_ref[:, cols] += out

    block = min(BLOCK, dec_len)
    for q in range(dec_len // block):
        products(mine + q * block, block, q == 0)

    def arrive(d, i):
        at = lax.rem(t + T - d, T) * dec_len + i * 2 * W
        cols = pl.ds(aligned(at), 2 * W)
        pltpu.make_async_copy(
            white_ref.at[:, cols], white_ref.at[:, cols], bulk_recv.at[d - 1, i]
        ).wait()
        products(at, 2 * W)

    def arrivals(d, _):
        for i in order:
            arrive(d, i)
        return 0

    if T == 2:
        arrivals(1, 0)
    else:
        lax.fori_loop(1, T, arrivals, 0)

    for k in range(groups):
        block = acc_ref[:, k * W:(k + 1) * W].T * scale
        for step in range(STEPS):
            to = (step * LAGS + k * lags) * step_len
            size = tall if k < groups - 1 else step_len
            out_ref[to:to + size, :] = block[step * tall:step * tall + size, :]

    @pl.when(t < T - 1)
    def _():
        to_right.wait_send()

    @pl.when(t > 0)
    def _():
        to_left.wait_send()

    for g in range(T):
        each(half, lambda i: end_first(g, i))
    each(C - 1, lambda d: second(d).wait_send())
    for d in range(1, T):
        for i in range(half):
            bulk(d, i).wait_send()


def per_device(C, T, raw_strain, fir_taps, sources):
    rows, raw_len = raw_strain.shape
    dec_len = raw_len // DECIM
    nb = dec_len // W
    half = nb * C // (T * nb)
    step_len = sources.shape[1] // T
    ns = STEPS * step_len
    total = T * dec_len
    groups = 2 * HALF_LAG // (W // ns) + 1
    bf, f32 = jnp.bfloat16, jnp.float32
    flat = pl.pallas_call(
        functools.partial(kernel, C, T, 1.0 / math.sqrt(total)),
        out_shape=pltpu.VMEM((STEPS * LAGS * step_len, rows), f32),
        in_specs=[
            pl.BlockSpec(memory_space=pltpu.HBM),
            pl.BlockSpec(memory_space=pltpu.HBM),
            pl.BlockSpec(memory_space=pltpu.HBM),
        ],
        out_specs=pl.BlockSpec(memory_space=pltpu.VMEM),
        scratch_shapes=[
            pltpu.VMEM((1, TAPS), bf),
            pltpu.SMEM(sources.shape, jnp.int32),
            pltpu.VMEM((rows, LEFT + raw_len + RIGHT), bf),
            pltpu.VMEM((rows, dec_len), f32),
            pltpu.VMEM((rows, dec_len + 2 * W), bf),
            pltpu.VMEM((rows, dec_len + 2 * W), bf),
            pltpu.VMEM((rows, total), bf),
            pltpu.VMEM((T * half + 1, 16, W), bf),
            pltpu.VMEM((C, 16, W), bf),
            pltpu.VMEM((C, 16, W), bf),
            pltpu.VMEM(((2 * C + 1) * STEPS * SLAB, 2 * W), f32),
            pltpu.VMEM((2 * W, W // ns * step_len // SLAB * W), bf),
            pltpu.VMEM((total + 2 * W, W), bf),
            pltpu.VMEM((rows, groups * W), f32),
            pltpu.SemaphoreType.DMA((2,)),
            pltpu.SemaphoreType.DMA((half,)),
            pltpu.SemaphoreType.DMA((2,)),
            pltpu.SemaphoreType.DMA((2,)),
            pltpu.SemaphoreType.DMA((T * half,)),
            pltpu.SemaphoreType.DMA,
            pltpu.SemaphoreType.DMA((C,)),
            pltpu.SemaphoreType.DMA,
            pltpu.SemaphoreType.DMA((T, half)),
            pltpu.SemaphoreType.DMA((T, half)),
        ],
        compiler_params=pltpu.CompilerParams(
            collective_id=0, has_side_effects=True, vmem_limit_bytes=62 * 1024 * 1024
        ),
    )(raw_strain, fir_taps.reshape(1, TAPS), sources)
    return jnp.swapaxes(flat.reshape(STEPS, LAGS, step_len, rows), 1, 2)


def solution(mesh):
    C, T = mesh.shape["chan"], mesh.shape["tm"]
    return jax.shard_map(
        functools.partial(per_device, C, T),
        mesh=mesh,
        in_specs=(P("chan", "tm"), P(), P()),
        out_specs=P(None, "tm", None, "chan"),
        check_vma=False,
    )
```

```python
import functools
import math

import jax
import jax.numpy as jnp
from jax import lax
from jax.experimental import pallas as pl
from jax.experimental.pallas import tpu as pltpu
from jax.sharding import PartitionSpec as P

TAPS = 64
DECIM = 4
HALF_WIN = 32
LAGS = 257
HALF_LAG = 128
STEPS = 2
W = 128
SLAB = 8
LOCAL = 4
LEAD = 2
EAGER = True
AHEAD = (2, 2, 4, 6)
BLOCK = 1024
LEFT = 256
RIGHT = 128
MESH = pl.DeviceIdType.MESH


def nt(a, b):
    return lax.dot_general(
        a, b, (((1,), (1,)), ((), ())), preferred_element_type=jnp.float32
    )


def aligned(x):
    return pl.multiple_of(x, W)


def kernel(
    C, T, scale,
    raw_ref, taps_hbm, src_hbm, out_ref,
    taps_ref, src_ref, praw_ref, x_ref, dec_ref, hi_ref, lo_ref, white_ref, send1, recv1, part, recv2, mixed, recv3, window_ref, shift_ref, shifted, acc_ref,
    small_sem, load_sem, halo_send, halo_recv, s1_sem, r1_sem, s2_sem, r2_sem, s3_sem, r3_sem, bulk_send, bulk_recv,
):
    c = lax.axis_index("chan")
    t = lax.axis_index("tm")
    rows, raw_len = raw_ref.shape
    dec_len = raw_len // DECIM
    nb = dec_len // W
    half = nb // 2
    per = half // LOCAL
    step_len = src_hbm.shape[1] // T
    ns = STEPS * step_len
    total = T * dec_len
    mine = t * dec_len

    barrier = pltpu.get_barrier_semaphore()

    Z = C // LOCAL
    deck, l = c // LOCAL, lax.rem(c, LOCAL)
    near = LOCAL * T
    spot = l * T + t

    def beside(d):
        other = lax.rem(spot + d, near)
        return other // T, lax.rem(other, T)

    def along(d):
        return lax.rem(deck + d, Z) * LOCAL + l, t

    def greet_beside(d, _):
        to_l, to_t = beside(d)
        pl.semaphore_signal(
            barrier, inc=1, device_id=(deck * LOCAL + to_l, to_t), device_id_type=MESH
        )
        return 0

    def greet_along(d, _):
        pl.semaphore_signal(barrier, inc=1, device_id=along(d), device_id_type=MESH)
        return 0

    lax.fori_loop(1, Z, greet_along, 0)
    lax.fori_loop(1, near, greet_beside, 0)

    small = [
        pltpu.make_async_copy(taps_hbm, taps_ref, small_sem.at[0]),
        pltpu.make_async_copy(src_hbm, src_ref, small_sem.at[1]),
    ]
    for copy in small:
        copy.start()
    seg = raw_len // half
    loads = []
    for i in range(half):
        load = pltpu.make_async_copy(
            raw_ref.at[:, pl.ds(i * seg, seg)],
            x_ref.at[:, pl.ds(LEFT + i * seg, seg)],
            load_sem.at[i],
        )
        load.start()
        loads.append(load)

    to_right = pltpu.make_async_remote_copy(
        src_ref=raw_ref.at[:, pl.ds(raw_len - LEFT, LEFT)],
        dst_ref=x_ref.at[:, pl.ds(0, LEFT)],
        send_sem=halo_send.at[0], recv_sem=halo_recv.at[0],
        device_id=(c, lax.rem(t + 1, T)), device_id_type=MESH,
    )
    to_left = pltpu.make_async_remote_copy(
        src_ref=raw_ref.at[:, pl.ds(0, RIGHT)],
        dst_ref=x_ref.at[:, pl.ds(LEFT + raw_len, RIGHT)],
        send_sem=halo_send.at[1], recv_sem=halo_recv.at[1],
        device_id=(c, lax.rem(t + T - 1, T)), device_id_type=MESH,
    )

    pl.semaphore_wait(barrier, near - 1 + Z - 1)

    @pl.when(t < T - 1)
    def _():
        to_right.start()

    @pl.when(t > 0)
    def _():
        to_left.start()

    @pl.when(t == 0)
    def _():
        x_ref[:, 0:LEFT] = jnp.zeros((rows, LEFT), jnp.bfloat16)

    @pl.when(t == T - 1)
    def _():
        x_ref[:, LEFT + raw_len:] = jnp.zeros((rows, RIGHT), jnp.bfloat16)

    span = lax.broadcasted_iota(jnp.int32, (2 * W, 4 * W), 1) - W - lax.broadcasted_iota(
        jnp.int32, (2 * W, 4 * W), 0
    )
    band = jnp.where((span >= -HALF_WIN) & (span <= HALF_WIN), 1.0, 0.0).astype(jnp.bfloat16)

    for copy in small:
        copy.wait()

    taps = jnp.broadcast_to(taps_ref[...], (16, TAPS))
    place = lax.broadcasted_iota(jnp.int32, (TAPS, W), 1) == lax.rem(
        W - lax.broadcasted_iota(jnp.int32, (TAPS, W), 0), W
    )
    base = jnp.dot(
        taps, place.astype(jnp.float32).astype(jnp.bfloat16), preferred_element_type=jnp.float32
    )
    rolled = pltpu.roll(
        jnp.broadcast_to(base[0:1, :], (W, W)), 0, 1, stride=DECIM, stride_axis=0
    )
    row_id = lax.broadcasted_iota(jnp.int32, (W, W), 0)
    lane_id = lax.broadcasted_iota(jnp.int32, (W, W), 1)
    fts = []
    for jc in range(DECIM + 1):
        k = DECIM * row_id + W - W * jc - lane_id
        fts.append(jnp.where((k >= 0) & (k < W), rolled, 0.0).astype(jnp.bfloat16))
    ft = jnp.concatenate(fts, axis=1)

    pr = lax.broadcasted_iota(jnp.int32, (T * SLAB, rows), 0)
    pc = lax.broadcasted_iota(jnp.int32, (T * SLAB, rows), 1)
    picks = jnp.zeros((T * SLAB, rows), jnp.float32)
    for g in range(T):
        for step in range(STEPS):
            for p in range(step_len):
                local = src_ref[step, g * step_len + p] - c * rows
                hit = (pr == g * SLAB + step * step_len + p) & (pc == local)
                picks = jnp.where(hit, 1.0, picks)
    picks = picks.astype(jnp.bfloat16)

    def put_mag(b, d):
        mag = jnp.abs(d)
        hi = mag.astype(jnp.bfloat16)
        hi_ref[:, (b + 1) * W:(b + 2) * W] = hi
        lo_ref[:, (b + 1) * W:(b + 2) * W] = (mag - hi.astype(jnp.float32)).astype(jnp.bfloat16)

    def decimate(blocks):
        begins = [LEFT - W + b * DECIM * W for b in blocks]
        x = jnp.concatenate([x_ref[:, a:a + (DECIM + 1) * W] for a in begins], axis=0)
        d = nt(x, ft)
        for i, b in enumerate(blocks):
            mine_d = d[i * rows:(i + 1) * rows]
            dec_ref[:, b * W:(b + 1) * W] = mine_d
            put_mag(b, mine_d)

    def first(d):
        to_l, g = beside(d)
        return pltpu.make_async_remote_copy(
            src_ref=send1.at[g * LOCAL + to_l], dst_ref=recv1.at[t * LOCAL + l],
            send_sem=s1_sem.at[d - 1], recv_sem=r1_sem,
            device_id=(deck * LOCAL + to_l, g), device_id_type=MESH,
        )

    def second(d):
        return pltpu.make_async_remote_copy(
            src_ref=part, dst_ref=recv2.at[d - 1],
            send_sem=s2_sem.at[d - 1], recv_sem=r2_sem,
            device_id=along(d), device_id_type=MESH,
        )

    def third(d):
        return pltpu.make_async_remote_copy(
            src_ref=mixed, dst_ref=recv3.at[l],
            send_sem=s3_sem.at[d - 1], recv_sem=r3_sem,
            device_id=(deck * LOCAL + lax.rem(l + d, LOCAL), t), device_id_type=MESH,
        )

    def bulk(d, i):
        cols = pl.ds(aligned(mine + i * 2 * W), 2 * W)
        return pltpu.make_async_remote_copy(
            src_ref=white_ref.at[:, cols], dst_ref=white_ref.at[:, cols],
            send_sem=bulk_send.at[d - 1, i], recv_sem=bulk_recv.at[d - 1, i],
            device_id=(c, lax.rem(t + d, T)), device_id_type=MESH,
        )

    def whiten(pairs):
        cols = [slice(2 * p * W, (2 * p + 4) * W) for p in pairs]
        sums = nt(jnp.concatenate([hi_ref[:, q] for q in cols], axis=0), band) + nt(
            jnp.concatenate([lo_ref[:, q] for q in cols], axis=0), band
        )
        level = sums / (2 * HALF_WIN + 1) + 1e-05
        for i, p in enumerate(pairs):
            d = dec_ref[:, 2 * p * W:2 * (p + 1) * W]
            w = (d / level[i * rows:(i + 1) * rows]).astype(jnp.bfloat16)
            white_ref[:, pl.ds(aligned(mine + 2 * p * W), 2 * W)] = w

    def all_bulk(i):
        for d in range(1, T):
            bulk(d, i).start()

    def each(count, body):
        if count <= 16:
            for i in range(count):
                body(i)
            return

        def step(i, _):
            body(i)
            return 0

        lax.fori_loop(0, count, step, 0)

    order = list(range(1, half - 1)) + [0, half - 1]
    lead = order[:LEAD]
    inner = order[LEAD:half - 2]
    edge = order[half - 2:]

    def pick_raw(x):
        return jnp.dot(picks, x, preferred_element_type=jnp.float32).astype(jnp.bfloat16)

    ahead = (DECIM + 1) * W
    many = T * SLAB
    praw_ref[:, 0:ahead - LEFT] = jnp.zeros((many, ahead - LEFT), jnp.bfloat16)
    praw_ref[:, ahead + raw_len + RIGHT:] = jnp.zeros((many, DECIM * W - RIGHT), jnp.bfloat16)
    for i in range(half):
        loads[i].wait()
        praw_ref[:, ahead + i * seg:ahead + (i + 1) * seg] = pick_raw(
            x_ref[:, LEFT + i * seg:LEFT + (i + 1) * seg]
        )
    made = {}

    def filter_picks(blocks):
        d = nt(
            jnp.concatenate(
                [praw_ref[:, a:a + ahead] for a in [(b + 1) * DECIM * W for b in blocks]], axis=0
            ),
            ft,
        )
        for i, b in enumerate(blocks):
            mine_d = d[i * many:(i + 1) * many]
            mag = jnp.abs(mine_d)
            lane = lax.broadcasted_iota(jnp.int32, (many, W), 1)
            if b < 0:
                mag = jnp.where((t > 0) & (lane >= W - HALF_WIN), mag, 0.0)
            if b == nb:
                mag = jnp.where((t < T - 1) & (lane < HALF_WIN), mag, 0.0)
            hi = mag.astype(jnp.bfloat16)
            made[b] = mine_d, hi, (mag - hi.astype(jnp.float32)).astype(jnp.bfloat16)

    narrow = band[0:W, 0:3 * W]
    narrow = jnp.concatenate([narrow, narrow], axis=1)

    def whiten_picks(pairs):
        blocks = [b for p in pairs for b in (2 * p, 2 * p + 1)]
        wide = jnp.concatenate(
            [
                jnp.concatenate([made[b + k][m] for m in (1, 2) for k in (-1, 0, 1)], axis=1)
                for b in blocks
            ],
            axis=0,
        )
        level = nt(wide, narrow) / (2 * HALF_WIN + 1) + 1e-05
        d = jnp.concatenate([made[b][0] for b in blocks], axis=0) / level
        for i, p in enumerate(pairs):
            at = p % per * 2 * SLAB
            for g in range(T):
                send1[g * LOCAL + p // per, at:at + 2 * SLAB] = jnp.concatenate(
                    [
                        d[q * many + g * SLAB:q * many + (g + 1) * SLAB]
                        for q in (2 * i, 2 * i + 1)
                    ],
                    axis=0,
                ).astype(jnp.bfloat16)

    filter_picks(range(1, nb))
    whiten_picks(range(1, half - 1))
    split = 2 * LEAD + 3
    if EAGER:
        decimate(range(1, split))
        whiten(lead)

    @pl.when(t > 0)
    def _():
        to_right.wait_recv()

    @pl.when(t < T - 1)
    def _():
        to_left.wait_recv()

    praw_ref[:, ahead - LEFT:ahead] = pick_raw(x_ref[:, 0:LEFT])
    praw_ref[:, ahead + raw_len:ahead + raw_len + RIGHT] = pick_raw(x_ref[:, LEFT + raw_len:])
    filter_picks([-1, 0, nb])
    whiten_picks([0, half - 1])
    each(near - 1, lambda d: first(d + 1).start())
    pltpu.make_async_copy(
        send1.at[t * LOCAL + l], recv1.at[t * LOCAL + l], r1_sem
    ).start()
    if not EAGER:
        decimate(range(1, split))
        whiten(lead)
    for p in order[:AHEAD[0]]:
        all_bulk(p)
    decimate(range(split, nb))
    whiten(inner)
    for p in order[AHEAD[0]:AHEAD[1]]:
        all_bulk(p)
    decimate([0])
    past = nt(x_ref[:, 0:LEFT], ft[:, 3 * W:5 * W])
    keep = (t > 0) & (lax.broadcasted_iota(jnp.int32, (rows, W), 1) >= W - HALF_WIN)
    put_mag(-1, jnp.where(keep, past, 0.0))
    after = nt(x_ref[:, LEFT + raw_len - W:LEFT + raw_len + RIGHT], ft[:, 0:2 * W])
    keep = (t < T - 1) & (lax.broadcasted_iota(jnp.int32, (rows, W), 1) < HALF_WIN)
    put_mag(nb, jnp.where(keep, after, 0.0))
    whiten(edge)
    for p in order[AHEAD[1]:AHEAD[2]]:
        all_bulk(p)

    shifted[0:W, :] = jnp.zeros((W, W), jnp.bfloat16)
    lags = W // ns
    tall = lags * step_len
    tiles = tall // SLAB
    group = SLAB // step_len
    sample = lax.broadcasted_iota(jnp.int32, (2 * W, tiles * W), 0)
    place = lax.broadcasted_iota(jnp.int32, (2 * W, tiles * W), 1)
    shift = jnp.where(sample == W + place % W - place // W * group, 1.0, 0.0)
    shift_ref[...] = shift.astype(jnp.bfloat16)

    pltpu.make_async_copy(recv1, recv1, r1_sem).wait()
    for g in range(T):
        summed = recv1[g * LOCAL].astype(jnp.float32)
        for j in range(1, LOCAL):
            summed = summed + recv1[g * LOCAL + j].astype(jnp.float32)
        part[g] = summed.astype(jnp.bfloat16)
    each(Z - 1, lambda d: second(d + 1).start())
    for p in order[AHEAD[2]:AHEAD[3]]:
        all_bulk(p)
    pltpu.make_async_copy(recv2, recv2, r2_sem).wait()
    for g in range(T):
        summed = part[g].astype(jnp.float32)
        for j in range(Z - 1):
            summed = summed + recv2[j, g].astype(jnp.float32)
        mixed[g] = summed.astype(jnp.bfloat16)
    each(LOCAL - 1, lambda d: third(d + 1).start())
    pltpu.make_async_copy(mixed, recv3.at[l], r3_sem).start()
    for p in order[AHEAD[3]:]:
        all_bulk(p)
    pltpu.make_async_copy(recv3, recv3, r3_sem).wait()

    gathered = jnp.concatenate(
        [
            recv3[p // per, g, p % per * 2 * SLAB:(p % per + 1) * 2 * SLAB]
            for g in range(T)
            for p in range(half)
        ],
        axis=1,
    )
    spread_row = lax.broadcasted_iota(jnp.int32, (2 * STEPS * SLAB, 2 * SLAB), 0)
    spread_col = lax.broadcasted_iota(jnp.int32, (2 * STEPS * SLAB, 2 * SLAB), 1)
    wanted = (spread_row // (STEPS * SLAB)) * SLAB + (spread_row // SLAB % STEPS) * step_len + (
        spread_row % step_len
    )
    spread = jnp.where(spread_col == wanted, 1.0, 0.0).astype(jnp.bfloat16)
    rep = jnp.dot(spread, gathered, preferred_element_type=jnp.float32)
    low = lax.broadcasted_iota(jnp.int32, (SLAB, W), 0) // step_len
    lane = lax.broadcasted_iota(jnp.int32, (SLAB, W), 1)
    zero = jnp.zeros((SLAB, W), jnp.float32)
    before = [zero] * STEPS
    turned = [[zero] * group] * STEPS
    for q in range(T * nb + 1):
        for step in range(STEPS):
            if q < T * nb:
                top = (q % 2 * STEPS + step) * SLAB
                x = rep[top:top + SLAB, q // 2 * W:(q // 2 + 1) * W]
                turn = [x] + [pltpu.roll(x, k, 1) for k in range(1, group)]
            else:
                x, turn = zero, [zero] * group
            for k in range(1, group):
                x = jnp.where(
                    low == k, jnp.where(lane >= k, turn[k], turned[step][k]), x
                )
            turned = turned[:step] + [turn] + turned[step + 1:]
            at = (q * STEPS + step) * SLAB
            window_ref[at:at + SLAB, 0:W] = before[step]
            window_ref[at:at + SLAB, W:] = x
            before[step] = x
    batch = 12
    for q in range(0, T * nb + 1, batch):
        count = min(batch, T * nb + 1 - q)
        span = STEPS * SLAB
        moved = jnp.dot(
            window_ref[q * span:(q + count) * span, :].astype(jnp.bfloat16), shift_ref[...],
            preferred_element_type=jnp.float32,
        )
        for i in range(count):
            z = jnp.concatenate(
                [
                    moved[(i * STEPS + step) * SLAB:(i * STEPS + step + 1) * SLAB, v * W:(v + 1) * W]
                    for step in range(STEPS)
                    for v in range(tiles)
                ],
                axis=0,
            )
            shifted[(q + i + 1) * W:(q + i + 2) * W, :] = z.T.astype(jnp.bfloat16)

    groups = 2 * HALF_LAG // lags + 1

    def products(starts, count, fresh=False):
        w = jnp.concatenate([white_ref[:, pl.ds(aligned(n), count)] for n in starts], axis=1)
        for k in range(0, groups, 2):
            b = jnp.concatenate(
                [
                    jnp.concatenate(
                        [
                            shifted[
                                pl.ds(pl.multiple_of(n + 2 * HALF_LAG - lags * m, 16), count), :
                            ]
                            for m in range(k, min(k + 2, groups))
                        ],
                        axis=1,
                    )
                    for n in starts
                ],
                axis=0,
            )
            out = jnp.dot(w, b, preferred_element_type=jnp.float32)
            cols = slice(k * W, k * W + b.shape[1])
            if fresh:
                acc_ref[:, cols] = out
            else:
                acc_ref[:, cols] += out

    for q in range(0, dec_len, min(BLOCK, dec_len)):
        products([mine + q], min(BLOCK, dec_len), q == 0)

    def arrivals(d, _):
        begin = lax.rem(t + T - d, T) * dec_len
        for pairs in (order[:half - 2], edge):
            for i in pairs:
                cols = pl.ds(aligned(begin + i * 2 * W), 2 * W)
                pltpu.make_async_copy(
                    white_ref.at[:, cols], white_ref.at[:, cols], bulk_recv.at[d - 1, i]
                ).wait()
            if pairs[-1] - pairs[0] == len(pairs) - 1:
                products([begin + pairs[0] * 2 * W], len(pairs) * 2 * W)
            else:
                products([begin + i * 2 * W for i in pairs], 2 * W)
        return 0

    if T == 2:
        arrivals(1, 0)
    else:
        lax.fori_loop(1, T, arrivals, 0)

    for k in range(groups):
        block = acc_ref[:, k * W:(k + 1) * W].T * scale
        for step in range(STEPS):
            to = (step * LAGS + k * lags) * step_len
            size = tall if k < groups - 1 else step_len
            out_ref[to:to + size, :] = block[step * tall:step * tall + size, :]

    @pl.when(t < T - 1)
    def _():
        to_right.wait_send()

    @pl.when(t > 0)
    def _():
        to_left.wait_send()

    each(near - 1, lambda d: first(d + 1).wait_send())
    each(Z - 1, lambda d: second(d + 1).wait_send())
    each(LOCAL - 1, lambda d: third(d + 1).wait_send())
    for d in range(1, T):
        for i in range(half):
            bulk(d, i).wait_send()


def per_device(C, T, raw_strain, fir_taps, sources):
    rows, raw_len = raw_strain.shape
    dec_len = raw_len // DECIM
    nb = dec_len // W
    half = nb // 2
    tall = half // LOCAL * 2 * SLAB
    step_len = sources.shape[1] // T
    ns = STEPS * step_len
    total = T * dec_len
    groups = 2 * HALF_LAG // (W // ns) + 1
    bf, f32 = jnp.bfloat16, jnp.float32
    flat = pl.pallas_call(
        functools.partial(kernel, C, T, 1.0 / math.sqrt(total)),
        out_shape=pltpu.VMEM((STEPS * LAGS * step_len, rows), f32),
        in_specs=[
            pl.BlockSpec(memory_space=pltpu.HBM),
            pl.BlockSpec(memory_space=pltpu.HBM),
            pl.BlockSpec(memory_space=pltpu.HBM),
        ],
        out_specs=pl.BlockSpec(memory_space=pltpu.VMEM),
        scratch_shapes=[
            pltpu.VMEM((1, TAPS), bf),
            pltpu.SMEM(sources.shape, jnp.int32),
            pltpu.VMEM((T * SLAB, raw_len + (2 * DECIM + 1) * W), bf),
            pltpu.VMEM((rows, LEFT + raw_len + RIGHT), bf),
            pltpu.VMEM((rows, dec_len), f32),
            pltpu.VMEM((rows, dec_len + 2 * W), bf),
            pltpu.VMEM((rows, dec_len + 2 * W), bf),
            pltpu.VMEM((rows, total), bf),
            pltpu.VMEM((LOCAL * T, tall, W), bf),
            pltpu.VMEM((LOCAL * T, tall, W), bf),
            pltpu.VMEM((T, tall, W), bf),
            pltpu.VMEM((C // LOCAL - 1, T, tall, W), bf),
            pltpu.VMEM((T, tall, W), bf),
            pltpu.VMEM((LOCAL, T, tall, W), bf),
            pltpu.VMEM(((T * nb + 1) * STEPS * SLAB, 2 * W), f32),
            pltpu.VMEM((2 * W, W // ns * step_len // SLAB * W), bf),
            pltpu.VMEM((total + 2 * W, W), bf),
            pltpu.VMEM((rows, groups * W), f32),
            pltpu.SemaphoreType.DMA((2,)),
            pltpu.SemaphoreType.DMA((half,)),
            pltpu.SemaphoreType.DMA((2,)),
            pltpu.SemaphoreType.DMA((2,)),
            pltpu.SemaphoreType.DMA((LOCAL * T - 1,)),
            pltpu.SemaphoreType.DMA,
            pltpu.SemaphoreType.DMA((C // LOCAL - 1,)),
            pltpu.SemaphoreType.DMA,
            pltpu.SemaphoreType.DMA((LOCAL - 1,)),
            pltpu.SemaphoreType.DMA,
            pltpu.SemaphoreType.DMA((T, half)),
            pltpu.SemaphoreType.DMA((T, half)),
        ],
        compiler_params=pltpu.CompilerParams(
            collective_id=0, has_side_effects=True, vmem_limit_bytes=62 * 1024 * 1024
        ),
    )(raw_strain, fir_taps.reshape(1, TAPS), sources)
    return jnp.swapaxes(flat.reshape(STEPS, LAGS, step_len, rows), 1, 2)


def solution(mesh):
    C, T = mesh.shape["chan"], mesh.shape["tm"]
    return jax.shard_map(
        functools.partial(per_device, C, T),
        mesh=mesh,
        in_specs=(P("chan", "tm"), P(), P()),
        out_specs=P(None, "tm", None, "chan"),
        check_vma=False,
    )
```

```python
import functools
import math

import jax
import jax.numpy as jnp
from jax import lax
from jax.experimental import pallas as pl
from jax.experimental.pallas import tpu as pltpu
from jax.sharding import PartitionSpec as P

TAPS = 64
DECIM = 4
HALF_WIN = 32
LAGS = 257
HALF_LAG = 128
STEPS = 2
W = 128
SLAB = 8
LOCAL = 4
LEAD = 1
MARGIN = 384
AHEAD = (1, 2, 4, 6)
BLOCK = 1024
LEFT = 256
RIGHT = 128
MESH = pl.DeviceIdType.MESH


def nt(a, b):
    return lax.dot_general(
        a, b, (((1,), (1,)), ((), ())), preferred_element_type=jnp.float32
    )


def aligned(x):
    return pl.multiple_of(x, W)


def kernel(
    C, T, scale,
    raw_ref, taps_hbm, src_hbm, out_ref,
    taps_ref, src_ref, praw_ref, x_ref, dec_ref, hi_ref, lo_ref, white_ref, send0, recv0, send1, recv1, part, recv2, mixed, recv3, window_ref, shift_ref, shifted, acc_ref,
    small_sem, load_sem, halo_send, halo_recv, s0_sem, r0_sem, s1_sem, r1_sem, s2_sem, r2_sem, s3_sem, r3_sem, bulk_send, bulk_recv,
):
    c = lax.axis_index("chan")
    t = lax.axis_index("tm")
    rows, raw_len = raw_ref.shape
    dec_len = raw_len // DECIM
    nb = dec_len // W
    half = nb // 2
    per = half // LOCAL
    step_len = src_hbm.shape[1] // T
    ns = STEPS * step_len
    total = T * dec_len
    mine = t * dec_len

    barrier = pltpu.get_barrier_semaphore()

    Z = C // LOCAL
    deck, l = c // LOCAL, lax.rem(c, LOCAL)
    near = LOCAL * T
    spot = l * T + t

    def beside(d):
        other = lax.rem(spot + d, near)
        return other // T, lax.rem(other, T)

    def along(d):
        return lax.rem(deck + d, Z) * LOCAL + l, t

    def greet_beside(d, _):
        to_l, to_t = beside(d)
        pl.semaphore_signal(
            barrier, inc=1, device_id=(deck * LOCAL + to_l, to_t), device_id_type=MESH
        )
        return 0

    def greet_along(d, _):
        pl.semaphore_signal(barrier, inc=1, device_id=along(d), device_id_type=MESH)
        return 0

    lax.fori_loop(1, Z, greet_along, 0)
    lax.fori_loop(1, near, greet_beside, 0)

    small = [
        pltpu.make_async_copy(taps_hbm, taps_ref, small_sem.at[0]),
        pltpu.make_async_copy(src_hbm, src_ref, small_sem.at[1]),
    ]
    for copy in small:
        copy.start()
    seg = raw_len // half
    loads = []
    for i in range(half):
        load = pltpu.make_async_copy(
            raw_ref.at[:, pl.ds(i * seg, seg)],
            x_ref.at[:, pl.ds(LEFT + i * seg, seg)],
            load_sem.at[i],
        )
        load.start()
        loads.append(load)

    to_right = pltpu.make_async_remote_copy(
        src_ref=raw_ref.at[:, pl.ds(raw_len - LEFT, LEFT)],
        dst_ref=x_ref.at[:, pl.ds(0, LEFT)],
        send_sem=halo_send.at[0], recv_sem=halo_recv.at[0],
        device_id=(c, lax.rem(t + 1, T)), device_id_type=MESH,
    )
    to_left = pltpu.make_async_remote_copy(
        src_ref=raw_ref.at[:, pl.ds(0, RIGHT)],
        dst_ref=x_ref.at[:, pl.ds(LEFT + raw_len, RIGHT)],
        send_sem=halo_send.at[1], recv_sem=halo_recv.at[1],
        device_id=(c, lax.rem(t + T - 1, T)), device_id_type=MESH,
    )

    pl.semaphore_wait(barrier, near - 1 + Z - 1)

    @pl.when(t < T - 1)
    def _():
        to_right.start()

    @pl.when(t > 0)
    def _():
        to_left.start()

    @pl.when(t == 0)
    def _():
        x_ref[:, 0:LEFT] = jnp.zeros((rows, LEFT), jnp.bfloat16)

    @pl.when(t == T - 1)
    def _():
        x_ref[:, LEFT + raw_len:] = jnp.zeros((rows, RIGHT), jnp.bfloat16)

    span = lax.broadcasted_iota(jnp.int32, (2 * W, 4 * W), 1) - W - lax.broadcasted_iota(
        jnp.int32, (2 * W, 4 * W), 0
    )
    band = jnp.where((span >= -HALF_WIN) & (span <= HALF_WIN), 1.0, 0.0).astype(jnp.bfloat16)

    for copy in small:
        copy.wait()

    taps = jnp.broadcast_to(taps_ref[...], (16, TAPS))
    place = lax.broadcasted_iota(jnp.int32, (TAPS, W), 1) == lax.rem(
        W - lax.broadcasted_iota(jnp.int32, (TAPS, W), 0), W
    )
    base = jnp.dot(
        taps, place.astype(jnp.float32).astype(jnp.bfloat16), preferred_element_type=jnp.float32
    )
    rolled = pltpu.roll(
        jnp.broadcast_to(base[0:1, :], (W, W)), 0, 1, stride=DECIM, stride_axis=0
    )
    row_id = lax.broadcasted_iota(jnp.int32, (W, W), 0)
    lane_id = lax.broadcasted_iota(jnp.int32, (W, W), 1)
    fts = []
    for jc in range(DECIM + 1):
        k = DECIM * row_id + W - W * jc - lane_id
        fts.append(jnp.where((k >= 0) & (k < W), rolled, 0.0).astype(jnp.bfloat16))
    ft = jnp.concatenate(fts, axis=1)

    pr = lax.broadcasted_iota(jnp.int32, (T * SLAB, rows), 0)
    pc = lax.broadcasted_iota(jnp.int32, (T * SLAB, rows), 1)
    picks = jnp.zeros((T * SLAB, rows), jnp.float32)
    for g in range(T):
        for step in range(STEPS):
            for p in range(step_len):
                local = src_ref[step, g * step_len + p] - c * rows
                hit = (pr == g * SLAB + step * step_len + p) & (pc == local)
                picks = jnp.where(hit, 1.0, picks)
    picks = picks.astype(jnp.bfloat16)

    def put_mag(b, d):
        mag = jnp.abs(d)
        hi = mag.astype(jnp.bfloat16)
        hi_ref[:, (b + 1) * W:(b + 2) * W] = hi
        lo_ref[:, (b + 1) * W:(b + 2) * W] = (mag - hi.astype(jnp.float32)).astype(jnp.bfloat16)

    def decimate(blocks):
        begins = [LEFT - W + b * DECIM * W for b in blocks]
        x = jnp.concatenate([x_ref[:, a:a + (DECIM + 1) * W] for a in begins], axis=0)
        d = nt(x, ft)
        for i, b in enumerate(blocks):
            mine_d = d[i * rows:(i + 1) * rows]
            dec_ref[:, b * W:(b + 1) * W] = mine_d
            put_mag(b, mine_d)

    def first(d):
        to_l, g = beside(d)
        return pltpu.make_async_remote_copy(
            src_ref=send1.at[g * LOCAL + to_l], dst_ref=recv1.at[t * LOCAL + l],
            send_sem=s1_sem.at[d - 1], recv_sem=r1_sem,
            device_id=(deck * LOCAL + to_l, g), device_id_type=MESH,
        )

    def second(d):
        return pltpu.make_async_remote_copy(
            src_ref=part, dst_ref=recv2.at[d - 1],
            send_sem=s2_sem.at[d - 1], recv_sem=r2_sem,
            device_id=along(d), device_id_type=MESH,
        )

    def third(d):
        return pltpu.make_async_remote_copy(
            src_ref=mixed, dst_ref=recv3.at[l],
            send_sem=s3_sem.at[d - 1], recv_sem=r3_sem,
            device_id=(deck * LOCAL + lax.rem(l + d, LOCAL), t), device_id_type=MESH,
        )

    def bulk(d, i):
        cols = pl.ds(aligned(mine + i * 2 * W), 2 * W)
        return pltpu.make_async_remote_copy(
            src_ref=white_ref.at[:, cols], dst_ref=white_ref.at[:, cols],
            send_sem=bulk_send.at[d - 1, i], recv_sem=bulk_recv.at[d - 1, i],
            device_id=(c, lax.rem(t + d, T)), device_id_type=MESH,
        )

    def whiten(pairs):
        cols = [slice(2 * p * W, (2 * p + 4) * W) for p in pairs]
        sums = nt(jnp.concatenate([hi_ref[:, q] for q in cols], axis=0), band) + nt(
            jnp.concatenate([lo_ref[:, q] for q in cols], axis=0), band
        )
        level = sums / (2 * HALF_WIN + 1) + 1e-05
        for i, p in enumerate(pairs):
            d = dec_ref[:, 2 * p * W:2 * (p + 1) * W]
            w = (d / level[i * rows:(i + 1) * rows]).astype(jnp.bfloat16)
            white_ref[:, pl.ds(aligned(mine + 2 * p * W), 2 * W)] = w

    def all_bulk(i):
        for d in range(1, T):
            bulk(d, i).start()

    def each(count, body):
        if count <= 16:
            for i in range(count):
                body(i)
            return

        def step(i, _):
            body(i)
            return 0

        lax.fori_loop(0, count, step, 0)

    order = list(range(1, half - 1)) + [0, half - 1]
    lead = order[:LEAD]
    inner = order[LEAD:half - 2]
    edge = order[half - 2:]

    def pick_raw(x):
        return jnp.dot(picks, x, preferred_element_type=jnp.float32)

    def split_mag(d):
        mag = jnp.abs(d)
        hi = mag.astype(jnp.bfloat16)
        return hi, (mag - hi.astype(jnp.float32)).astype(jnp.bfloat16)

    narrow = band[0:W, 0:3 * W]
    narrow = jnp.concatenate([narrow, narrow], axis=1)

    def divide(d, wide):
        return d / (nt(wide, narrow) / (2 * HALF_WIN + 1) + 1e-05)

    ahead = (DECIM + 1) * W
    many = T * SLAB
    praw_ref[:, 0:ahead] = jnp.zeros((many, ahead), jnp.bfloat16)
    for i in range(half):
        loads[i].wait()
        x = pick_raw(x_ref[:, LEFT + i * seg:LEFT + (i + 1) * seg])
        praw_ref[:, ahead + i * seg:ahead + (i + 1) * seg] = x.astype(jnp.bfloat16)
        for kind, which, begin in ((0, half - 1, seg - MARGIN), (1, 0, 0)):
            if i == which:
                for g in range(T):
                    send0[kind, g] = jnp.concatenate(
                        [
                            x[g * SLAB:(g + 1) * SLAB, begin + k * W:begin + (k + 1) * W]
                            for k in range(MARGIN // W)
                        ]
                        + [jnp.zeros((SLAB, W), jnp.float32)],
                        axis=0,
                    ).astype(jnp.bfloat16)

    def outer(kind, e, g):
        to_l = e * (LOCAL - 1)
        slot = jnp.where(kind == 0, t, t - 1)
        inside = t < T - 1 if kind == 0 else t > 0
        same = (to_l == l) & (g == t)
        copy = pltpu.make_async_remote_copy(
            src_ref=send0.at[kind, g], dst_ref=recv0.at[kind, slot, l],
            send_sem=s0_sem.at[kind, e, g], recv_sem=r0_sem,
            device_id=(deck * LOCAL + to_l, g), device_id_type=MESH,
        )
        own = pltpu.make_async_copy(send0.at[kind, g], recv0.at[kind, slot, l], r0_sem)
        return inside & jnp.logical_not(same), inside & same, copy, own

    outers = [(kind, e, g) for kind in range(2) for e in range(2) for g in range(T)]

    def start_outer(kind, e, g):
        away, here, copy, own = outer(kind, e, g)

        @pl.when(away)
        def _():
            copy.start()

        @pl.when(here)
        def _():
            own.start()

    def end_outer(kind, e, g):
        away, here, copy, own = outer(kind, e, g)

        @pl.when(away)
        def _():
            copy.wait_send()

    for which in outers:
        start_outer(*which)

    d = nt(
        jnp.concatenate(
            [praw_ref[:, a:a + ahead] for a in [(b + 1) * DECIM * W for b in range(nb)]], axis=0
        ),
        ft,
    )
    none = jnp.zeros((many, W), jnp.bfloat16)
    mags = [jnp.concatenate([none, m, none], axis=0) for m in split_mag(d)]
    d = divide(
        d,
        jnp.concatenate(
            [m[k * many:(k + nb) * many] for m in mags for k in range(3)], axis=1
        ),
    )
    for p in range(half):
        at = p % per * 2 * SLAB
        for g in range(T):
            send1[g * LOCAL + p // per, at:at + 2 * SLAB] = jnp.concatenate(
                [
                    d[q * many + g * SLAB:q * many + (g + 1) * SLAB]
                    for q in (2 * p, 2 * p + 1)
                ],
                axis=0,
            ).astype(jnp.bfloat16)
    each(near - 1, lambda d: first(d + 1).start())
    pltpu.make_async_copy(
        send1.at[t * LOCAL + l], recv1.at[t * LOCAL + l], r1_sem
    ).start()
    split = 2 * LEAD + 3
    decimate(range(1, split))
    whiten(lead)
    for p in order[:AHEAD[0]]:
        all_bulk(p)
    decimate(range(split, nb))
    whiten(inner)
    for p in order[AHEAD[0]:AHEAD[1]]:
        all_bulk(p)

    @pl.when(t > 0)
    def _():
        to_right.wait_recv()

    @pl.when(t < T - 1)
    def _():
        to_left.wait_recv()

    decimate([0])
    past = nt(x_ref[:, 0:LEFT], ft[:, 3 * W:5 * W])
    keep = (t > 0) & (lax.broadcasted_iota(jnp.int32, (rows, W), 1) >= W - HALF_WIN)
    put_mag(-1, jnp.where(keep, past, 0.0))
    after = nt(x_ref[:, LEFT + raw_len - W:LEFT + raw_len + RIGHT], ft[:, 0:2 * W])
    keep = (t < T - 1) & (lax.broadcasted_iota(jnp.int32, (rows, W), 1) < HALF_WIN)
    put_mag(nb, jnp.where(keep, after, 0.0))
    whiten(edge)
    for p in order[AHEAD[1]:AHEAD[2]]:
        all_bulk(p)

    shifted[0:W, :] = jnp.zeros((W, W), jnp.bfloat16)
    lags = W // ns
    tall = lags * step_len
    tiles = tall // SLAB
    group = SLAB // step_len
    sample = lax.broadcasted_iota(jnp.int32, (2 * W, tiles * W), 0)
    place = lax.broadcasted_iota(jnp.int32, (2 * W, tiles * W), 1)
    shift = jnp.where(sample == W + place % W - place // W * group, 1.0, 0.0)
    shift_ref[...] = shift.astype(jnp.bfloat16)

    pltpu.make_async_copy(recv1, recv1, r1_sem).wait()
    for g in range(T):
        summed = recv1[g * LOCAL].astype(jnp.float32)
        for j in range(1, LOCAL):
            summed = summed + recv1[g * LOCAL + j].astype(jnp.float32)
        part[g] = summed.astype(jnp.bfloat16)

    @pl.when((l == 0) | (l == LOCAL - 1))
    def _():
        pltpu.make_async_copy(recv0, recv0, r0_sem).wait()
        row = lax.broadcasted_iota(jnp.int32, (2 * SLAB, W), 0)
        lane = lax.broadcasted_iota(jnp.int32, (2 * SLAB, W), 1)
        blank = jnp.zeros((SLAB, W), jnp.float32)
        for g in range(T - 1):
            tiles = []
            for kind in range(2):
                summed = recv0[kind, g, 0].astype(jnp.float32)
                for j in range(1, LOCAL):
                    summed = summed + recv0[kind, g, j].astype(jnp.float32)
                tiles += [summed[k * SLAB:(k + 1) * SLAB] for k in range(MARGIN // W)]
            raws = [[blank, blank] + tiles[0:3], tiles[2:6] + [blank]]
            d = nt(
                jnp.concatenate(
                    [jnp.concatenate(r, axis=1) for r in raws], axis=0
                ).astype(jnp.bfloat16),
                ft,
            )
            wide = []
            for m in split_mag(d):
                m = m.astype(jnp.float32)
                left, right = m[0:SLAB], m[SLAB:]
                wide += [
                    jnp.concatenate(pair, axis=0)
                    for pair in ((blank, left), (left, right), (right, blank))
                ]
            d = divide(d, jnp.concatenate(wide, axis=1).astype(jnp.bfloat16))
            swap = jnp.concatenate([d[SLAB:], d[0:SLAB]], axis=0)

            @pl.when(l == LOCAL - 1)
            def _():
                old = part[g, 2 * SLAB * (per - 1):2 * SLAB * per].astype(jnp.float32)
                edge_row = (row >= SLAB) & (lane >= W - HALF_WIN)
                part[g, 2 * SLAB * (per - 1):2 * SLAB * per] = jnp.where(
                    edge_row, swap, old
                ).astype(jnp.bfloat16)

            @pl.when(l == 0)
            def _():
                old = part[g + 1, 0:2 * SLAB].astype(jnp.float32)
                edge_row = (row < SLAB) & (lane < HALF_WIN + TAPS // DECIM)
                part[g + 1, 0:2 * SLAB] = jnp.where(edge_row, swap, old).astype(jnp.bfloat16)

    each(Z - 1, lambda d: second(d + 1).start())
    for p in order[AHEAD[2]:AHEAD[3]]:
        all_bulk(p)
    pltpu.make_async_copy(recv2, recv2, r2_sem).wait()
    for g in range(T):
        summed = part[g].astype(jnp.float32)
        for j in range(Z - 1):
            summed = summed + recv2[j, g].astype(jnp.float32)
        mixed[g] = summed.astype(jnp.bfloat16)
    each(LOCAL - 1, lambda d: third(d + 1).start())
    pltpu.make_async_copy(mixed, recv3.at[l], r3_sem).start()
    for p in order[AHEAD[3]:]:
        all_bulk(p)
    pltpu.make_async_copy(recv3, recv3, r3_sem).wait()

    gathered = jnp.concatenate(
        [
            recv3[p // per, g, p % per * 2 * SLAB:(p % per + 1) * 2 * SLAB]
            for g in range(T)
            for p in range(half)
        ],
        axis=1,
    )
    spread_row = lax.broadcasted_iota(jnp.int32, (2 * STEPS * SLAB, 2 * SLAB), 0)
    spread_col = lax.broadcasted_iota(jnp.int32, (2 * STEPS * SLAB, 2 * SLAB), 1)
    wanted = (spread_row // (STEPS * SLAB)) * SLAB + (spread_row // SLAB % STEPS) * step_len + (
        spread_row % step_len
    )
    spread = jnp.where(spread_col == wanted, 1.0, 0.0).astype(jnp.bfloat16)
    rep = jnp.dot(spread, gathered, preferred_element_type=jnp.float32)
    low = lax.broadcasted_iota(jnp.int32, (SLAB, W), 0) // step_len
    lane = lax.broadcasted_iota(jnp.int32, (SLAB, W), 1)
    zero = jnp.zeros((SLAB, W), jnp.float32)
    before = [zero] * STEPS
    turned = [[zero] * group] * STEPS
    for q in range(T * nb + 1):
        for step in range(STEPS):
            if q < T * nb:
                top = (q % 2 * STEPS + step) * SLAB
                x = rep[top:top + SLAB, q // 2 * W:(q // 2 + 1) * W]
                turn = [x] + [pltpu.roll(x, k, 1) for k in range(1, group)]
            else:
                x, turn = zero, [zero] * group
            for k in range(1, group):
                x = jnp.where(
                    low == k, jnp.where(lane >= k, turn[k], turned[step][k]), x
                )
            turned = turned[:step] + [turn] + turned[step + 1:]
            at = (q * STEPS + step) * SLAB
            window_ref[at:at + SLAB, 0:W] = before[step]
            window_ref[at:at + SLAB, W:] = x
            before[step] = x
    batch = 12
    for q in range(0, T * nb + 1, batch):
        count = min(batch, T * nb + 1 - q)
        span = STEPS * SLAB
        moved = jnp.dot(
            window_ref[q * span:(q + count) * span, :].astype(jnp.bfloat16), shift_ref[...],
            preferred_element_type=jnp.float32,
        )
        for i in range(count):
            z = jnp.concatenate(
                [
                    moved[(i * STEPS + step) * SLAB:(i * STEPS + step + 1) * SLAB, v * W:(v + 1) * W]
                    for step in range(STEPS)
                    for v in range(tiles)
                ],
                axis=0,
            )
            shifted[(q + i + 1) * W:(q + i + 2) * W, :] = z.T.astype(jnp.bfloat16)

    groups = 2 * HALF_LAG // lags + 1

    def products(starts, count, fresh=False):
        w = jnp.concatenate([white_ref[:, pl.ds(aligned(n), count)] for n in starts], axis=1)
        for k in range(0, groups, 2):
            b = jnp.concatenate(
                [
                    jnp.concatenate(
                        [
                            shifted[
                                pl.ds(pl.multiple_of(n + 2 * HALF_LAG - lags * m, 16), count), :
                            ]
                            for m in range(k, min(k + 2, groups))
                        ],
                        axis=1,
                    )
                    for n in starts
                ],
                axis=0,
            )
            out = jnp.dot(w, b, preferred_element_type=jnp.float32)
            cols = slice(k * W, k * W + b.shape[1])
            if fresh:
                acc_ref[:, cols] = out
            else:
                acc_ref[:, cols] += out

    for q in range(0, dec_len, min(BLOCK, dec_len)):
        products([mine + q], min(BLOCK, dec_len), q == 0)

    def arrivals(d, _):
        begin = lax.rem(t + T - d, T) * dec_len
        for pairs in (order[:half - 2], edge):
            for i in pairs:
                cols = pl.ds(aligned(begin + i * 2 * W), 2 * W)
                pltpu.make_async_copy(
                    white_ref.at[:, cols], white_ref.at[:, cols], bulk_recv.at[d - 1, i]
                ).wait()
            if pairs[-1] - pairs[0] == len(pairs) - 1:
                products([begin + pairs[0] * 2 * W], len(pairs) * 2 * W)
            else:
                products([begin + i * 2 * W for i in pairs], 2 * W)
        return 0

    if T == 2:
        arrivals(1, 0)
    else:
        lax.fori_loop(1, T, arrivals, 0)

    for k in range(groups):
        block = acc_ref[:, k * W:(k + 1) * W].T * scale
        for step in range(STEPS):
            to = (step * LAGS + k * lags) * step_len
            size = tall if k < groups - 1 else step_len
            out_ref[to:to + size, :] = block[step * tall:step * tall + size, :]

    @pl.when(t < T - 1)
    def _():
        to_right.wait_send()

    @pl.when(t > 0)
    def _():
        to_left.wait_send()

    for which in outers:
        end_outer(*which)
    each(near - 1, lambda d: first(d + 1).wait_send())
    each(Z - 1, lambda d: second(d + 1).wait_send())
    each(LOCAL - 1, lambda d: third(d + 1).wait_send())
    for d in range(1, T):
        for i in range(half):
            bulk(d, i).wait_send()


def per_device(C, T, raw_strain, fir_taps, sources):
    rows, raw_len = raw_strain.shape
    dec_len = raw_len // DECIM
    nb = dec_len // W
    half = nb // 2
    tall = half // LOCAL * 2 * SLAB
    margin = (MARGIN // W + 1) * SLAB
    step_len = sources.shape[1] // T
    ns = STEPS * step_len
    total = T * dec_len
    groups = 2 * HALF_LAG // (W // ns) + 1
    bf, f32 = jnp.bfloat16, jnp.float32
    flat = pl.pallas_call(
        functools.partial(kernel, C, T, 1.0 / math.sqrt(total)),
        out_shape=pltpu.VMEM((STEPS * LAGS * step_len, rows), f32),
        in_specs=[
            pl.BlockSpec(memory_space=pltpu.HBM),
            pl.BlockSpec(memory_space=pltpu.HBM),
            pl.BlockSpec(memory_space=pltpu.HBM),
        ],
        out_specs=pl.BlockSpec(memory_space=pltpu.VMEM),
        scratch_shapes=[
            pltpu.VMEM((1, TAPS), bf),
            pltpu.SMEM(sources.shape, jnp.int32),
            pltpu.VMEM((T * SLAB, raw_len + (2 * DECIM + 1) * W), bf),
            pltpu.VMEM((rows, LEFT + raw_len + RIGHT), bf),
            pltpu.VMEM((rows, dec_len), f32),
            pltpu.VMEM((rows, dec_len + 2 * W), bf),
            pltpu.VMEM((rows, dec_len + 2 * W), bf),
            pltpu.VMEM((rows, total), bf),
            pltpu.VMEM((2, T, margin, W), bf),
            pltpu.VMEM((2, T - 1, LOCAL, margin, W), bf),
            pltpu.VMEM((LOCAL * T, tall, W), bf),
            pltpu.VMEM((LOCAL * T, tall, W), bf),
            pltpu.VMEM((T, tall, W), bf),
            pltpu.VMEM((C // LOCAL - 1, T, tall, W), bf),
            pltpu.VMEM((T, tall, W), bf),
            pltpu.VMEM((LOCAL, T, tall, W), bf),
            pltpu.VMEM(((T * nb + 1) * STEPS * SLAB, 2 * W), f32),
            pltpu.VMEM((2 * W, W // ns * step_len // SLAB * W), bf),
            pltpu.VMEM((total + 2 * W, W), bf),
            pltpu.VMEM((rows, groups * W), f32),
            pltpu.SemaphoreType.DMA((2,)),
            pltpu.SemaphoreType.DMA((half,)),
            pltpu.SemaphoreType.DMA((2,)),
            pltpu.SemaphoreType.DMA((2,)),
            pltpu.SemaphoreType.DMA((2, 2, T)),
            pltpu.SemaphoreType.DMA,
            pltpu.SemaphoreType.DMA((LOCAL * T - 1,)),
            pltpu.SemaphoreType.DMA,
            pltpu.SemaphoreType.DMA((C // LOCAL - 1,)),
            pltpu.SemaphoreType.DMA,
            pltpu.SemaphoreType.DMA((LOCAL - 1,)),
            pltpu.SemaphoreType.DMA,
            pltpu.SemaphoreType.DMA((T, half)),
            pltpu.SemaphoreType.DMA((T, half)),
        ],
        compiler_params=pltpu.CompilerParams(
            collective_id=0, has_side_effects=True, vmem_limit_bytes=62 * 1024 * 1024
        ),
    )(raw_strain, fir_taps.reshape(1, TAPS), sources)
    return jnp.swapaxes(flat.reshape(STEPS, LAGS, step_len, rows), 1, 2)


def solution(mesh):
    C, T = mesh.shape["chan"], mesh.shape["tm"]
    return jax.shard_map(
        functools.partial(per_device, C, T),
        mesh=mesh,
        in_specs=(P("chan", "tm"), P(), P()),
        out_specs=P(None, "tm", None, "chan"),
        check_vma=False,
    )
```

```python
import functools
import math

import jax
import jax.numpy as jnp
from jax import lax
from jax.experimental import pallas as pl
from jax.experimental.pallas import tpu as pltpu
from jax.sharding import PartitionSpec as P

TAPS = 64
DECIM = 4
HALF_WIN = 32
LAGS = 257
HALF_LAG = 128
STEPS = 2
W = 128
SLAB = 8
LOCAL = 4
LEAD = 1
MARGIN = 384
PRE = 1
AHEAD = (1, 2, 4, 6)
BLOCK = 1024
LEFT = 256
RIGHT = 128
MESH = pl.DeviceIdType.MESH


def nt(a, b):
    return lax.dot_general(
        a, b, (((1,), (1,)), ((), ())), preferred_element_type=jnp.float32
    )


def aligned(x):
    return pl.multiple_of(x, W)


def kernel(
    C, T, scale,
    raw_ref, taps_hbm, src_hbm, out_ref,
    taps_ref, src_ref, praw_ref, x_ref, dec_ref, hi_ref, lo_ref, white_ref, send0, recv0, send1, recv1, part, recv2, mixed, recv3, window_ref, shift_ref, shifted, acc_ref,
    small_sem, load_sem, halo_send, halo_recv, s0_sem, r0_sem, s1_sem, r1_sem, s2_sem, r2_sem, s3_sem, r3_sem, bulk_send, bulk_recv,
):
    c = lax.axis_index("chan")
    t = lax.axis_index("tm")
    rows, raw_len = raw_ref.shape
    dec_len = raw_len // DECIM
    nb = dec_len // W
    half = nb // 2
    per = half // LOCAL
    step_len = src_hbm.shape[1] // T
    ns = STEPS * step_len
    total = T * dec_len
    mine = t * dec_len

    barrier = pltpu.get_barrier_semaphore()

    Z = C // LOCAL
    deck, l = c // LOCAL, lax.rem(c, LOCAL)
    near = LOCAL * T
    spot = l * T + t

    def beside(d):
        other = lax.rem(spot + d, near)
        return other // T, lax.rem(other, T)

    def along(d):
        return lax.rem(deck + d, Z) * LOCAL + l, t

    def greet_beside(d, _):
        to_l, to_t = beside(d)
        pl.semaphore_signal(
            barrier, inc=1, device_id=(deck * LOCAL + to_l, to_t), device_id_type=MESH
        )
        return 0

    def greet_along(d, _):
        pl.semaphore_signal(barrier, inc=1, device_id=along(d), device_id_type=MESH)
        return 0

    lax.fori_loop(1, Z, greet_along, 0)
    lax.fori_loop(1, near, greet_beside, 0)

    small = [
        pltpu.make_async_copy(taps_hbm, taps_ref, small_sem.at[0]),
        pltpu.make_async_copy(src_hbm, src_ref, small_sem.at[1]),
    ]
    for copy in small:
        copy.start()
    seg = raw_len // half
    loads = []
    for i in range(half):
        load = pltpu.make_async_copy(
            raw_ref.at[:, pl.ds(i * seg, seg)],
            x_ref.at[:, pl.ds(LEFT + i * seg, seg)],
            load_sem.at[i],
        )
        load.start()
        loads.append(load)

    to_right = pltpu.make_async_remote_copy(
        src_ref=raw_ref.at[:, pl.ds(raw_len - LEFT, LEFT)],
        dst_ref=x_ref.at[:, pl.ds(0, LEFT)],
        send_sem=halo_send.at[0], recv_sem=halo_recv.at[0],
        device_id=(c, lax.rem(t + 1, T)), device_id_type=MESH,
    )
    to_left = pltpu.make_async_remote_copy(
        src_ref=raw_ref.at[:, pl.ds(0, RIGHT)],
        dst_ref=x_ref.at[:, pl.ds(LEFT + raw_len, RIGHT)],
        send_sem=halo_send.at[1], recv_sem=halo_recv.at[1],
        device_id=(c, lax.rem(t + T - 1, T)), device_id_type=MESH,
    )

    pl.semaphore_wait(barrier, near - 1 + Z - 1)

    @pl.when(t < T - 1)
    def _():
        to_right.start()

    @pl.when(t > 0)
    def _():
        to_left.start()

    @pl.when(t == 0)
    def _():
        x_ref[:, 0:LEFT] = jnp.zeros((rows, LEFT), jnp.bfloat16)

    @pl.when(t == T - 1)
    def _():
        x_ref[:, LEFT + raw_len:] = jnp.zeros((rows, RIGHT), jnp.bfloat16)

    span = lax.broadcasted_iota(jnp.int32, (2 * W, 4 * W), 1) - W - lax.broadcasted_iota(
        jnp.int32, (2 * W, 4 * W), 0
    )
    band = jnp.where((span >= -HALF_WIN) & (span <= HALF_WIN), 1.0, 0.0).astype(jnp.bfloat16)

    for copy in small:
        copy.wait()

    taps = jnp.broadcast_to(taps_ref[...], (16, TAPS))
    place = lax.broadcasted_iota(jnp.int32, (TAPS, W), 1) == lax.rem(
        W - lax.broadcasted_iota(jnp.int32, (TAPS, W), 0), W
    )
    base = jnp.dot(
        taps, place.astype(jnp.float32).astype(jnp.bfloat16), preferred_element_type=jnp.float32
    )
    rolled = pltpu.roll(
        jnp.broadcast_to(base[0:1, :], (W, W)), 0, 1, stride=DECIM, stride_axis=0
    )
    row_id = lax.broadcasted_iota(jnp.int32, (W, W), 0)
    lane_id = lax.broadcasted_iota(jnp.int32, (W, W), 1)
    fts = []
    for jc in range(DECIM + 1):
        k = DECIM * row_id + W - W * jc - lane_id
        fts.append(jnp.where((k >= 0) & (k < W), rolled, 0.0).astype(jnp.bfloat16))
    ft = jnp.concatenate(fts, axis=1)

    pr = lax.broadcasted_iota(jnp.int32, (T * SLAB, rows), 0)
    pc = lax.broadcasted_iota(jnp.int32, (T * SLAB, rows), 1)
    picks = jnp.zeros((T * SLAB, rows), jnp.float32)
    for g in range(T):
        for step in range(STEPS):
            for p in range(step_len):
                local = src_ref[step, g * step_len + p] - c * rows
                hit = (pr == g * SLAB + step * step_len + p) & (pc == local)
                picks = jnp.where(hit, 1.0, picks)
    picks = picks.astype(jnp.bfloat16)

    def put_mag(b, d):
        mag = jnp.abs(d)
        hi = mag.astype(jnp.bfloat16)
        hi_ref[:, (b + 1) * W:(b + 2) * W] = hi
        lo_ref[:, (b + 1) * W:(b + 2) * W] = (mag - hi.astype(jnp.float32)).astype(jnp.bfloat16)

    def decimate(blocks):
        begins = [LEFT - W + b * DECIM * W for b in blocks]
        x = jnp.concatenate([x_ref[:, a:a + (DECIM + 1) * W] for a in begins], axis=0)
        d = nt(x, ft)
        for i, b in enumerate(blocks):
            mine_d = d[i * rows:(i + 1) * rows]
            dec_ref[:, b * W:(b + 1) * W] = mine_d
            put_mag(b, mine_d)

    def first(d):
        to_l, g = beside(d)
        return pltpu.make_async_remote_copy(
            src_ref=send1.at[g * LOCAL + to_l], dst_ref=recv1.at[t * LOCAL + l],
            send_sem=s1_sem.at[d - 1], recv_sem=r1_sem,
            device_id=(deck * LOCAL + to_l, g), device_id_type=MESH,
        )

    def second(d):
        return pltpu.make_async_remote_copy(
            src_ref=part, dst_ref=recv2.at[d - 1],
            send_sem=s2_sem.at[d - 1], recv_sem=r2_sem,
            device_id=along(d), device_id_type=MESH,
        )

    def third(d):
        return pltpu.make_async_remote_copy(
            src_ref=mixed, dst_ref=recv3.at[l],
            send_sem=s3_sem.at[d - 1], recv_sem=r3_sem,
            device_id=(deck * LOCAL + lax.rem(l + d, LOCAL), t), device_id_type=MESH,
        )

    def bulk(d, i):
        cols = pl.ds(aligned(mine + i * 2 * W), 2 * W)
        return pltpu.make_async_remote_copy(
            src_ref=white_ref.at[:, cols], dst_ref=white_ref.at[:, cols],
            send_sem=bulk_send.at[d - 1, i], recv_sem=bulk_recv.at[d - 1, i],
            device_id=(c, lax.rem(t + d, T)), device_id_type=MESH,
        )

    def whiten(pairs):
        cols = [slice(2 * p * W, (2 * p + 4) * W) for p in pairs]
        sums = nt(jnp.concatenate([hi_ref[:, q] for q in cols], axis=0), band) + nt(
            jnp.concatenate([lo_ref[:, q] for q in cols], axis=0), band
        )
        level = sums / (2 * HALF_WIN + 1) + 1e-05
        for i, p in enumerate(pairs):
            d = dec_ref[:, 2 * p * W:2 * (p + 1) * W]
            w = (d / level[i * rows:(i + 1) * rows]).astype(jnp.bfloat16)
            white_ref[:, pl.ds(aligned(mine + 2 * p * W), 2 * W)] = w

    def all_bulk(i):
        for d in range(1, T):
            bulk(d, i).start()

    def each(count, body):
        if count <= 16:
            for i in range(count):
                body(i)
            return

        def step(i, _):
            body(i)
            return 0

        lax.fori_loop(0, count, step, 0)

    order = list(range(1, half - 1)) + [0, half - 1]
    lead = order[:LEAD]
    inner = order[LEAD:half - 2]
    edge = order[half - 2:]

    def pick_raw(x):
        return jnp.dot(picks, x, preferred_element_type=jnp.float32)

    def split_mag(d):
        mag = jnp.abs(d)
        hi = mag.astype(jnp.bfloat16)
        return hi, (mag - hi.astype(jnp.float32)).astype(jnp.bfloat16)

    narrow = band[0:W, 0:3 * W]
    narrow = jnp.concatenate([narrow, narrow], axis=1)

    def divide(d, wide):
        return d / (nt(wide, narrow) / (2 * HALF_WIN + 1) + 1e-05)

    split = 2 * LEAD + 3
    soon = -(-split // 2)
    for i in range(soon):
        loads[i].wait()
    decimate(range(1, split))
    whiten(lead)
    for p in order[:PRE]:
        all_bulk(p)

    ahead = (DECIM + 1) * W
    many = T * SLAB
    praw_ref[:, 0:ahead] = jnp.zeros((many, ahead), jnp.bfloat16)
    for i in range(half):
        if i >= soon:
            loads[i].wait()
        x = pick_raw(x_ref[:, LEFT + i * seg:LEFT + (i + 1) * seg])
        praw_ref[:, ahead + i * seg:ahead + (i + 1) * seg] = x.astype(jnp.bfloat16)
        for kind, which, begin in ((0, half - 1, seg - MARGIN), (1, 0, 0)):
            if i == which:
                for g in range(T):
                    send0[kind, g] = jnp.concatenate(
                        [
                            x[g * SLAB:(g + 1) * SLAB, begin + k * W:begin + (k + 1) * W]
                            for k in range(MARGIN // W)
                        ]
                        + [jnp.zeros((SLAB, W), jnp.float32)],
                        axis=0,
                    ).astype(jnp.bfloat16)

    def outer(kind, e, g):
        to_l = e * (LOCAL - 1)
        slot = jnp.where(kind == 0, t, t - 1)
        inside = t < T - 1 if kind == 0 else t > 0
        same = (to_l == l) & (g == t)
        copy = pltpu.make_async_remote_copy(
            src_ref=send0.at[kind, g], dst_ref=recv0.at[kind, slot, l],
            send_sem=s0_sem.at[kind, e, g], recv_sem=r0_sem,
            device_id=(deck * LOCAL + to_l, g), device_id_type=MESH,
        )
        own = pltpu.make_async_copy(send0.at[kind, g], recv0.at[kind, slot, l], r0_sem)
        return inside & jnp.logical_not(same), inside & same, copy, own

    outers = [(kind, e, g) for kind in range(2) for e in range(2) for g in range(T)]

    def start_outer(kind, e, g):
        away, here, copy, own = outer(kind, e, g)

        @pl.when(away)
        def _():
            copy.start()

        @pl.when(here)
        def _():
            own.start()

    def end_outer(kind, e, g):
        away, here, copy, own = outer(kind, e, g)

        @pl.when(away)
        def _():
            copy.wait_send()

    for which in outers:
        start_outer(*which)

    d = nt(
        jnp.concatenate(
            [praw_ref[:, a:a + ahead] for a in [(b + 1) * DECIM * W for b in range(nb)]], axis=0
        ),
        ft,
    )
    none = jnp.zeros((many, W), jnp.bfloat16)
    mags = [jnp.concatenate([none, m, none], axis=0) for m in split_mag(d)]
    d = divide(
        d,
        jnp.concatenate(
            [m[k * many:(k + nb) * many] for m in mags for k in range(3)], axis=1
        ),
    )
    for p in range(half):
        at = p % per * 2 * SLAB
        for g in range(T):
            send1[g * LOCAL + p // per, at:at + 2 * SLAB] = jnp.concatenate(
                [
                    d[q * many + g * SLAB:q * many + (g + 1) * SLAB]
                    for q in (2 * p, 2 * p + 1)
                ],
                axis=0,
            ).astype(jnp.bfloat16)
    each(near - 1, lambda d: first(d + 1).start())
    pltpu.make_async_copy(
        send1.at[t * LOCAL + l], recv1.at[t * LOCAL + l], r1_sem
    ).start()
    for p in order[PRE:AHEAD[0]]:
        all_bulk(p)
    decimate(range(split, nb))
    whiten(inner)
    for p in order[AHEAD[0]:AHEAD[1]]:
        all_bulk(p)

    @pl.when(t > 0)
    def _():
        to_right.wait_recv()

    @pl.when(t < T - 1)
    def _():
        to_left.wait_recv()

    decimate([0])
    past = nt(x_ref[:, 0:LEFT], ft[:, 3 * W:5 * W])
    keep = (t > 0) & (lax.broadcasted_iota(jnp.int32, (rows, W), 1) >= W - HALF_WIN)
    put_mag(-1, jnp.where(keep, past, 0.0))
    after = nt(x_ref[:, LEFT + raw_len - W:LEFT + raw_len + RIGHT], ft[:, 0:2 * W])
    keep = (t < T - 1) & (lax.broadcasted_iota(jnp.int32, (rows, W), 1) < HALF_WIN)
    put_mag(nb, jnp.where(keep, after, 0.0))
    whiten(edge)
    for p in order[AHEAD[1]:AHEAD[2]]:
        all_bulk(p)

    shifted[0:W, :] = jnp.zeros((W, W), jnp.bfloat16)
    lags = W // ns
    tall = lags * step_len
    tiles = tall // SLAB
    group = SLAB // step_len
    sample = lax.broadcasted_iota(jnp.int32, (2 * W, tiles * W), 0)
    place = lax.broadcasted_iota(jnp.int32, (2 * W, tiles * W), 1)
    shift = jnp.where(sample == W + place % W - place // W * group, 1.0, 0.0)
    shift_ref[...] = shift.astype(jnp.bfloat16)

    pltpu.make_async_copy(recv1, recv1, r1_sem).wait()
    for g in range(T):
        summed = recv1[g * LOCAL].astype(jnp.float32)
        for j in range(1, LOCAL):
            summed = summed + recv1[g * LOCAL + j].astype(jnp.float32)
        part[g] = summed.astype(jnp.bfloat16)

    @pl.when((l == 0) | (l == LOCAL - 1))
    def _():
        pltpu.make_async_copy(recv0, recv0, r0_sem).wait()
        row = lax.broadcasted_iota(jnp.int32, (2 * SLAB, W), 0)
        lane = lax.broadcasted_iota(jnp.int32, (2 * SLAB, W), 1)
        blank = jnp.zeros((SLAB, W), jnp.float32)
        for g in range(T - 1):
            tiles = []
            for kind in range(2):
                summed = recv0[kind, g, 0].astype(jnp.float32)
                for j in range(1, LOCAL):
                    summed = summed + recv0[kind, g, j].astype(jnp.float32)
                tiles += [summed[k * SLAB:(k + 1) * SLAB] for k in range(MARGIN // W)]
            raws = [[blank, blank] + tiles[0:3], tiles[2:6] + [blank]]
            d = nt(
                jnp.concatenate(
                    [jnp.concatenate(r, axis=1) for r in raws], axis=0
                ).astype(jnp.bfloat16),
                ft,
            )
            wide = []
            for m in split_mag(d):
                m = m.astype(jnp.float32)
                left, right = m[0:SLAB], m[SLAB:]
                wide += [
                    jnp.concatenate(pair, axis=0)
                    for pair in ((blank, left), (left, right), (right, blank))
                ]
            d = divide(d, jnp.concatenate(wide, axis=1).astype(jnp.bfloat16))
            swap = jnp.concatenate([d[SLAB:], d[0:SLAB]], axis=0)

            @pl.when(l == LOCAL - 1)
            def _():
                old = part[g, 2 * SLAB * (per - 1):2 * SLAB * per].astype(jnp.float32)
                edge_row = (row >= SLAB) & (lane >= W - HALF_WIN)
                part[g, 2 * SLAB * (per - 1):2 * SLAB * per] = jnp.where(
                    edge_row, swap, old
                ).astype(jnp.bfloat16)

            @pl.when(l == 0)
            def _():
                old = part[g + 1, 0:2 * SLAB].astype(jnp.float32)
                edge_row = (row < SLAB) & (lane < HALF_WIN + TAPS // DECIM)
                part[g + 1, 0:2 * SLAB] = jnp.where(edge_row, swap, old).astype(jnp.bfloat16)

    each(Z - 1, lambda d: second(d + 1).start())
    for p in order[AHEAD[2]:AHEAD[3]]:
        all_bulk(p)
    pltpu.make_async_copy(recv2, recv2, r2_sem).wait()
    for g in range(T):
        summed = part[g].astype(jnp.float32)
        for j in range(Z - 1):
            summed = summed + recv2[j, g].astype(jnp.float32)
        mixed[g] = summed.astype(jnp.bfloat16)
    each(LOCAL - 1, lambda d: third(d + 1).start())
    pltpu.make_async_copy(mixed, recv3.at[l], r3_sem).start()
    for p in order[AHEAD[3]:]:
        all_bulk(p)
    pltpu.make_async_copy(recv3, recv3, r3_sem).wait()

    gathered = jnp.concatenate(
        [
            recv3[p // per, g, p % per * 2 * SLAB:(p % per + 1) * 2 * SLAB]
            for g in range(T)
            for p in range(half)
        ],
        axis=1,
    )
    spread_row = lax.broadcasted_iota(jnp.int32, (2 * STEPS * SLAB, 2 * SLAB), 0)
    spread_col = lax.broadcasted_iota(jnp.int32, (2 * STEPS * SLAB, 2 * SLAB), 1)
    wanted = (spread_row // (STEPS * SLAB)) * SLAB + (spread_row // SLAB % STEPS) * step_len + (
        spread_row % step_len
    )
    spread = jnp.where(spread_col == wanted, 1.0, 0.0).astype(jnp.bfloat16)
    rep = jnp.dot(spread, gathered, preferred_element_type=jnp.float32)
    low = lax.broadcasted_iota(jnp.int32, (SLAB, W), 0) // step_len
    lane = lax.broadcasted_iota(jnp.int32, (SLAB, W), 1)
    zero = jnp.zeros((SLAB, W), jnp.float32)
    before = [zero] * STEPS
    turned = [[zero] * group] * STEPS
    for q in range(T * nb + 1):
        for step in range(STEPS):
            if q < T * nb:
                top = (q % 2 * STEPS + step) * SLAB
                x = rep[top:top + SLAB, q // 2 * W:(q // 2 + 1) * W]
                turn = [x] + [pltpu.roll(x, k, 1) for k in range(1, group)]
            else:
                x, turn = zero, [zero] * group
            for k in range(1, group):
                x = jnp.where(
                    low == k, jnp.where(lane >= k, turn[k], turned[step][k]), x
                )
            turned = turned[:step] + [turn] + turned[step + 1:]
            at = (q * STEPS + step) * SLAB
            window_ref[at:at + SLAB, 0:W] = before[step]
            window_ref[at:at + SLAB, W:] = x
            before[step] = x
    batch = 12
    for q in range(0, T * nb + 1, batch):
        count = min(batch, T * nb + 1 - q)
        span = STEPS * SLAB
        moved = jnp.dot(
            window_ref[q * span:(q + count) * span, :].astype(jnp.bfloat16), shift_ref[...],
            preferred_element_type=jnp.float32,
        )
        for i in range(count):
            z = jnp.concatenate(
                [
                    moved[(i * STEPS + step) * SLAB:(i * STEPS + step + 1) * SLAB, v * W:(v + 1) * W]
                    for step in range(STEPS)
                    for v in range(tiles)
                ],
                axis=0,
            )
            shifted[(q + i + 1) * W:(q + i + 2) * W, :] = z.T.astype(jnp.bfloat16)

    groups = 2 * HALF_LAG // lags + 1

    def products(starts, count, fresh=False):
        w = jnp.concatenate([white_ref[:, pl.ds(aligned(n), count)] for n in starts], axis=1)
        for k in range(0, groups, 2):
            b = jnp.concatenate(
                [
                    jnp.concatenate(
                        [
                            shifted[
                                pl.ds(pl.multiple_of(n + 2 * HALF_LAG - lags * m, 16), count), :
                            ]
                            for m in range(k, min(k + 2, groups))
                        ],
                        axis=1,
                    )
                    for n in starts
                ],
                axis=0,
            )
            out = jnp.dot(w, b, preferred_element_type=jnp.float32)
            cols = slice(k * W, k * W + b.shape[1])
            if fresh:
                acc_ref[:, cols] = out
            else:
                acc_ref[:, cols] += out

    for q in range(0, dec_len, min(BLOCK, dec_len)):
        products([mine + q], min(BLOCK, dec_len), q == 0)

    def arrivals(d, _):
        begin = lax.rem(t + T - d, T) * dec_len
        for pairs in (order[:half - 2], edge):
            for i in pairs:
                cols = pl.ds(aligned(begin + i * 2 * W), 2 * W)
                pltpu.make_async_copy(
                    white_ref.at[:, cols], white_ref.at[:, cols], bulk_recv.at[d - 1, i]
                ).wait()
            if pairs[-1] - pairs[0] == len(pairs) - 1:
                products([begin + pairs[0] * 2 * W], len(pairs) * 2 * W)
            else:
                products([begin + i * 2 * W for i in pairs], 2 * W)
        return 0

    if T == 2:
        arrivals(1, 0)
    else:
        lax.fori_loop(1, T, arrivals, 0)

    for k in range(groups):
        block = acc_ref[:, k * W:(k + 1) * W].T * scale
        for step in range(STEPS):
            to = (step * LAGS + k * lags) * step_len
            size = tall if k < groups - 1 else step_len
            out_ref[to:to + size, :] = block[step * tall:step * tall + size, :]

    @pl.when(t < T - 1)
    def _():
        to_right.wait_send()

    @pl.when(t > 0)
    def _():
        to_left.wait_send()

    for which in outers:
        end_outer(*which)
    each(near - 1, lambda d: first(d + 1).wait_send())
    each(Z - 1, lambda d: second(d + 1).wait_send())
    each(LOCAL - 1, lambda d: third(d + 1).wait_send())
    for d in range(1, T):
        for i in range(half):
            bulk(d, i).wait_send()


def per_device(C, T, raw_strain, fir_taps, sources):
    rows, raw_len = raw_strain.shape
    dec_len = raw_len // DECIM
    nb = dec_len // W
    half = nb // 2
    tall = half // LOCAL * 2 * SLAB
    margin = (MARGIN // W + 1) * SLAB
    step_len = sources.shape[1] // T
    ns = STEPS * step_len
    total = T * dec_len
    groups = 2 * HALF_LAG // (W // ns) + 1
    bf, f32 = jnp.bfloat16, jnp.float32
    flat = pl.pallas_call(
        functools.partial(kernel, C, T, 1.0 / math.sqrt(total)),
        out_shape=pltpu.VMEM((STEPS * LAGS * step_len, rows), f32),
        in_specs=[
            pl.BlockSpec(memory_space=pltpu.HBM),
            pl.BlockSpec(memory_space=pltpu.HBM),
            pl.BlockSpec(memory_space=pltpu.HBM),
        ],
        out_specs=pl.BlockSpec(memory_space=pltpu.VMEM),
        scratch_shapes=[
            pltpu.VMEM((1, TAPS), bf),
            pltpu.SMEM(sources.shape, jnp.int32),
            pltpu.VMEM((T * SLAB, raw_len + (2 * DECIM + 1) * W), bf),
            pltpu.VMEM((rows, LEFT + raw_len + RIGHT), bf),
            pltpu.VMEM((rows, dec_len), f32),
            pltpu.VMEM((rows, dec_len + 2 * W), bf),
            pltpu.VMEM((rows, dec_len + 2 * W), bf),
            pltpu.VMEM((rows, total), bf),
            pltpu.VMEM((2, T, margin, W), bf),
            pltpu.VMEM((2, T - 1, LOCAL, margin, W), bf),
            pltpu.VMEM((LOCAL * T, tall, W), bf),
            pltpu.VMEM((LOCAL * T, tall, W), bf),
            pltpu.VMEM((T, tall, W), bf),
            pltpu.VMEM((C // LOCAL - 1, T, tall, W), bf),
            pltpu.VMEM((T, tall, W), bf),
            pltpu.VMEM((LOCAL, T, tall, W), bf),
            pltpu.VMEM(((T * nb + 1) * STEPS * SLAB, 2 * W), f32),
            pltpu.VMEM((2 * W, W // ns * step_len // SLAB * W), bf),
            pltpu.VMEM((total + 2 * W, W), bf),
            pltpu.VMEM((rows, groups * W), f32),
            pltpu.SemaphoreType.DMA((2,)),
            pltpu.SemaphoreType.DMA((half,)),
            pltpu.SemaphoreType.DMA((2,)),
            pltpu.SemaphoreType.DMA((2,)),
            pltpu.SemaphoreType.DMA((2, 2, T)),
            pltpu.SemaphoreType.DMA,
            pltpu.SemaphoreType.DMA((LOCAL * T - 1,)),
            pltpu.SemaphoreType.DMA,
            pltpu.SemaphoreType.DMA((C // LOCAL - 1,)),
            pltpu.SemaphoreType.DMA,
            pltpu.SemaphoreType.DMA((LOCAL - 1,)),
            pltpu.SemaphoreType.DMA,
            pltpu.SemaphoreType.DMA((T, half)),
            pltpu.SemaphoreType.DMA((T, half)),
        ],
        compiler_params=pltpu.CompilerParams(
            collective_id=0, has_side_effects=True, vmem_limit_bytes=62 * 1024 * 1024
        ),
    )(raw_strain, fir_taps.reshape(1, TAPS), sources)
    return jnp.swapaxes(flat.reshape(STEPS, LAGS, step_len, rows), 1, 2)


def solution(mesh):
    C, T = mesh.shape["chan"], mesh.shape["tm"]
    return jax.shard_map(
        functools.partial(per_device, C, T),
        mesh=mesh,
        in_specs=(P("chan", "tm"), P(), P()),
        out_specs=P(None, "tm", None, "chan"),
        check_vma=False,
    )
```

```python
import functools
import math

import jax
import jax.numpy as jnp
from jax import lax
from jax.experimental import pallas as pl
from jax.experimental.pallas import tpu as pltpu
from jax.sharding import PartitionSpec as P

TAPS = 64
DECIM = 4
HALF_WIN = 32
LAGS = 257
HALF_LAG = 128
STEPS = 2
W = 128
SLAB = 8
LOCAL = 4
LEAD = 1
MARGIN = 384
PRE = 1
AHEAD = (1, 2, 4, 6)
BLOCK = 1024
LEFT = 256
RIGHT = 128
MESH = pl.DeviceIdType.MESH


def nt(a, b):
    return lax.dot_general(
        a, b, (((1,), (1,)), ((), ())), preferred_element_type=jnp.float32
    )


def aligned(x):
    return pl.multiple_of(x, W)


def kernel(
    C, T, scale,
    raw_ref, taps_hbm, src_hbm, out_ref,
    taps_ref, src_ref, praw_ref, x_ref, dec_ref, hi_ref, lo_ref, white_ref, send0, recv0, send1, recv1, part, recv2, mixed, recv3, window_ref, shift_ref, shifted, acc_ref, line_ref, far_ref,
    small_sem, load_sem, halo_send, halo_recv, s0_sem, r0_sem, s1_sem, r1_sem, s2_sem, r2_sem, s3_sem, r3_sem, bulk_send, bulk_recv,
):
    c = lax.axis_index("chan")
    t = lax.axis_index("tm")
    rows, raw_len = raw_ref.shape
    dec_len = raw_len // DECIM
    nb = dec_len // W
    half = nb // 2
    per = half // LOCAL
    step_len = src_hbm.shape[1] // T
    ns = STEPS * step_len
    total = T * dec_len
    mine = t * dec_len

    barrier = pltpu.get_barrier_semaphore()

    Z = C // LOCAL
    deck, l = c // LOCAL, lax.rem(c, LOCAL)
    near = LOCAL * T
    spot = l * T + t

    def beside(d):
        other = lax.rem(spot + d, near)
        return other // T, lax.rem(other, T)

    def along(d):
        return lax.rem(deck + d, Z) * LOCAL + l, t

    def greet_beside(d, _):
        to_l, to_t = beside(d)
        pl.semaphore_signal(
            barrier, inc=1, device_id=(deck * LOCAL + to_l, to_t), device_id_type=MESH
        )
        return 0

    def greet_along(d, _):
        pl.semaphore_signal(barrier, inc=1, device_id=along(d), device_id_type=MESH)
        return 0

    lax.fori_loop(1, Z, greet_along, 0)
    lax.fori_loop(1, near, greet_beside, 0)

    small = [
        pltpu.make_async_copy(taps_hbm, taps_ref, small_sem.at[0]),
        pltpu.make_async_copy(src_hbm, src_ref, small_sem.at[1]),
    ]
    for copy in small:
        copy.start()
    seg = raw_len // half
    loads = []
    for i in range(half):
        load = pltpu.make_async_copy(
            raw_ref.at[:, pl.ds(i * seg, seg)],
            x_ref.at[:, pl.ds(LEFT + i * seg, seg)],
            load_sem.at[i],
        )
        load.start()
        loads.append(load)

    to_right = pltpu.make_async_remote_copy(
        src_ref=raw_ref.at[:, pl.ds(raw_len - LEFT, LEFT)],
        dst_ref=x_ref.at[:, pl.ds(0, LEFT)],
        send_sem=halo_send.at[0], recv_sem=halo_recv.at[0],
        device_id=(c, lax.rem(t + 1, T)), device_id_type=MESH,
    )
    to_left = pltpu.make_async_remote_copy(
        src_ref=raw_ref.at[:, pl.ds(0, RIGHT)],
        dst_ref=x_ref.at[:, pl.ds(LEFT + raw_len, RIGHT)],
        send_sem=halo_send.at[1], recv_sem=halo_recv.at[1],
        device_id=(c, lax.rem(t + T - 1, T)), device_id_type=MESH,
    )

    @pl.when(t == 0)
    def _():
        x_ref[:, 0:LEFT] = jnp.zeros((rows, LEFT), jnp.bfloat16)

    @pl.when(t == T - 1)
    def _():
        x_ref[:, LEFT + raw_len:] = jnp.zeros((rows, RIGHT), jnp.bfloat16)

    span = lax.broadcasted_iota(jnp.int32, (2 * W, 4 * W), 1) - W - lax.broadcasted_iota(
        jnp.int32, (2 * W, 4 * W), 0
    )
    band = jnp.where((span >= -HALF_WIN) & (span <= HALF_WIN), 1.0, 0.0).astype(jnp.bfloat16)

    for copy in small:
        copy.wait()

    taps = jnp.broadcast_to(taps_ref[...], (16, TAPS))
    place = lax.broadcasted_iota(jnp.int32, (TAPS, W), 1) == lax.rem(
        W - lax.broadcasted_iota(jnp.int32, (TAPS, W), 0), W
    )
    base = jnp.dot(
        taps, place.astype(jnp.float32).astype(jnp.bfloat16), preferred_element_type=jnp.float32
    )
    rolled = pltpu.roll(
        jnp.broadcast_to(base[0:1, :], (W, W)), 0, 1, stride=DECIM, stride_axis=0
    )
    row_id = lax.broadcasted_iota(jnp.int32, (W, W), 0)
    lane_id = lax.broadcasted_iota(jnp.int32, (W, W), 1)
    fts = []
    for jc in range(DECIM + 1):
        k = DECIM * row_id + W - W * jc - lane_id
        fts.append(jnp.where((k >= 0) & (k < W), rolled, 0.0).astype(jnp.bfloat16))
    ft = jnp.concatenate(fts, axis=1)

    pr = lax.broadcasted_iota(jnp.int32, (T * SLAB, rows), 0)
    pc = lax.broadcasted_iota(jnp.int32, (T * SLAB, rows), 1)
    picks = jnp.zeros((T * SLAB, rows), jnp.float32)
    for g in range(T):
        for step in range(STEPS):
            for p in range(step_len):
                local = src_ref[step, g * step_len + p] - c * rows
                hit = (pr == g * SLAB + step * step_len + p) & (pc == local)
                picks = jnp.where(hit, 1.0, picks)
    picks = picks.astype(jnp.bfloat16)

    def put_mag(b, d):
        mag = jnp.abs(d)
        hi = mag.astype(jnp.bfloat16)
        hi_ref[:, (b + 1) * W:(b + 2) * W] = hi
        lo_ref[:, (b + 1) * W:(b + 2) * W] = (mag - hi.astype(jnp.float32)).astype(jnp.bfloat16)

    def decimate(blocks):
        begins = [LEFT - W + b * DECIM * W for b in blocks]
        x = jnp.concatenate([x_ref[:, a:a + (DECIM + 1) * W] for a in begins], axis=0)
        d = nt(x, ft)
        for i, b in enumerate(blocks):
            mine_d = d[i * rows:(i + 1) * rows]
            dec_ref[:, b * W:(b + 1) * W] = mine_d
            put_mag(b, mine_d)

    def first(d):
        to_l, g = beside(d)
        return pltpu.make_async_remote_copy(
            src_ref=send1.at[g * LOCAL + to_l], dst_ref=recv1.at[t * LOCAL + l],
            send_sem=s1_sem.at[d - 1], recv_sem=r1_sem,
            device_id=(deck * LOCAL + to_l, g), device_id_type=MESH,
        )

    def second(d):
        return pltpu.make_async_remote_copy(
            src_ref=part, dst_ref=recv2.at[d - 1],
            send_sem=s2_sem.at[d - 1], recv_sem=r2_sem,
            device_id=along(d), device_id_type=MESH,
        )

    def third(d):
        return pltpu.make_async_remote_copy(
            src_ref=mixed, dst_ref=recv3.at[l],
            send_sem=s3_sem.at[d - 1], recv_sem=r3_sem,
            device_id=(deck * LOCAL + lax.rem(l + d, LOCAL), t), device_id_type=MESH,
        )

    def bulk(d, i):
        cols = pl.ds(aligned(mine + i * 2 * W), 2 * W)
        return pltpu.make_async_remote_copy(
            src_ref=white_ref.at[:, cols], dst_ref=white_ref.at[:, cols],
            send_sem=bulk_send.at[d - 1, i], recv_sem=bulk_recv.at[d - 1, i],
            device_id=(c, lax.rem(t + d, T)), device_id_type=MESH,
        )

    def whiten(pairs):
        cols = [slice(2 * p * W, (2 * p + 4) * W) for p in pairs]
        sums = nt(jnp.concatenate([hi_ref[:, q] for q in cols], axis=0), band) + nt(
            jnp.concatenate([lo_ref[:, q] for q in cols], axis=0), band
        )
        level = sums / (2 * HALF_WIN + 1) + 1e-05
        for i, p in enumerate(pairs):
            d = dec_ref[:, 2 * p * W:2 * (p + 1) * W]
            w = (d / level[i * rows:(i + 1) * rows]).astype(jnp.bfloat16)
            white_ref[:, pl.ds(aligned(mine + 2 * p * W), 2 * W)] = w

    def all_bulk(i):
        for d in range(1, T):
            bulk(d, i).start()

    def each(count, body):
        if count <= 16:
            for i in range(count):
                body(i)
            return

        def step(i, _):
            body(i)
            return 0

        lax.fori_loop(0, count, step, 0)

    order = list(range(1, half - 1)) + [0, half - 1]
    lead = order[:LEAD]
    inner = order[LEAD:half - 2]
    edge = order[half - 2:]

    def pick_raw(x):
        return jnp.dot(picks, x, preferred_element_type=jnp.float32)

    def split_mag(d):
        mag = jnp.abs(d)
        hi = mag.astype(jnp.bfloat16)
        return hi, (mag - hi.astype(jnp.float32)).astype(jnp.bfloat16)

    narrow = band[0:W, 0:3 * W]
    narrow = jnp.concatenate([narrow, narrow], axis=1)

    def divide(d, wide):
        return d / (nt(wide, narrow) / (2 * HALF_WIN + 1) + 1e-05)

    split = 2 * LEAD + 3
    soon = -(-split // 2)
    for i in range(soon):
        loads[i].wait()
    decimate(range(1, split))
    whiten(lead)
    pl.semaphore_wait(barrier, near - 1 + Z - 1)

    for p in order[:PRE]:
        all_bulk(p)

    ahead = (DECIM + 1) * W
    many = T * SLAB
    praw_ref[:, 0:ahead] = jnp.zeros((many, ahead), jnp.bfloat16)
    for i in range(half):
        if i >= soon:
            loads[i].wait()
        x = pick_raw(x_ref[:, LEFT + i * seg:LEFT + (i + 1) * seg])
        praw_ref[:, ahead + i * seg:ahead + (i + 1) * seg] = x.astype(jnp.bfloat16)
        for kind, which, begin in ((0, half - 1, seg - MARGIN), (1, 0, 0)):
            if i == which:
                for g in range(T):
                    send0[kind, g] = jnp.concatenate(
                        [
                            x[g * SLAB:(g + 1) * SLAB, begin + k * W:begin + (k + 1) * W]
                            for k in range(MARGIN // W)
                        ]
                        + [jnp.zeros((SLAB, W), jnp.float32)],
                        axis=0,
                    ).astype(jnp.bfloat16)

    def outer(kind, e, g):
        to_l = e * (LOCAL - 1)
        slot = jnp.where(kind == 0, t, t - 1)
        inside = t < T - 1 if kind == 0 else t > 0
        same = (to_l == l) & (g == t)
        copy = pltpu.make_async_remote_copy(
            src_ref=send0.at[kind, g], dst_ref=recv0.at[kind, slot, l],
            send_sem=s0_sem.at[kind, e, g], recv_sem=r0_sem,
            device_id=(deck * LOCAL + to_l, g), device_id_type=MESH,
        )
        own = pltpu.make_async_copy(send0.at[kind, g], recv0.at[kind, slot, l], r0_sem)
        return inside & jnp.logical_not(same), inside & same, copy, own

    outers = [(kind, e, g) for kind in range(2) for e in range(2) for g in range(T)]

    def start_outer(kind, e, g):
        away, here, copy, own = outer(kind, e, g)

        @pl.when(away)
        def _():
            copy.start()

        @pl.when(here)
        def _():
            own.start()

    def end_outer(kind, e, g):
        away, here, copy, own = outer(kind, e, g)

        @pl.when(away)
        def _():
            copy.wait_send()

    for which in outers:
        start_outer(*which)

    d = nt(
        jnp.concatenate(
            [praw_ref[:, a:a + ahead] for a in [(b + 1) * DECIM * W for b in range(nb)]], axis=0
        ),
        ft,
    )
    none = jnp.zeros((many, W), jnp.bfloat16)
    mags = [jnp.concatenate([none, m, none], axis=0) for m in split_mag(d)]
    d = divide(
        d,
        jnp.concatenate(
            [m[k * many:(k + nb) * many] for m in mags for k in range(3)], axis=1
        ),
    )
    for p in range(half):
        at = p % per * 2 * SLAB
        for g in range(T):
            send1[g * LOCAL + p // per, at:at + 2 * SLAB] = jnp.concatenate(
                [
                    d[q * many + g * SLAB:q * many + (g + 1) * SLAB]
                    for q in (2 * p, 2 * p + 1)
                ],
                axis=0,
            ).astype(jnp.bfloat16)
    each(near - 1, lambda d: first(d + 1).start())
    pltpu.make_async_copy(
        send1.at[t * LOCAL + l], recv1.at[t * LOCAL + l], r1_sem
    ).start()
    @pl.when(t < T - 1)
    def _():
        to_right.start()

    @pl.when(t > 0)
    def _():
        to_left.start()

    for p in order[PRE:AHEAD[0]]:
        all_bulk(p)
    decimate(range(split, nb))
    whiten(inner)
    for p in order[AHEAD[0]:AHEAD[1]]:
        all_bulk(p)
    for p in order[AHEAD[1]:AHEAD[2]]:
        all_bulk(p)

    shifted[0:W, :] = jnp.zeros((W, W), jnp.bfloat16)
    lags = W // ns
    tall = lags * step_len
    tiles = tall // SLAB
    group = SLAB // step_len
    sample = lax.broadcasted_iota(jnp.int32, (2 * W, tiles * W), 0)
    place = lax.broadcasted_iota(jnp.int32, (2 * W, tiles * W), 1)
    shift = jnp.where(sample == W + place % W - place // W * group, 1.0, 0.0)
    shift_ref[...] = shift.astype(jnp.bfloat16)

    pltpu.make_async_copy(recv1, recv1, r1_sem).wait()
    for g in range(T):
        summed = recv1[g * LOCAL].astype(jnp.float32)
        for j in range(1, LOCAL):
            summed = summed + recv1[g * LOCAL + j].astype(jnp.float32)
        part[g] = summed.astype(jnp.bfloat16)

    @pl.when((l == 0) | (l == LOCAL - 1))
    def _():
        pltpu.make_async_copy(recv0, recv0, r0_sem).wait()
        row = lax.broadcasted_iota(jnp.int32, (2 * SLAB, W), 0)
        lane = lax.broadcasted_iota(jnp.int32, (2 * SLAB, W), 1)
        blank = jnp.zeros((SLAB, W), jnp.float32)
        for g in range(T - 1):
            tiles = []
            for kind in range(2):
                summed = recv0[kind, g, 0].astype(jnp.float32)
                for j in range(1, LOCAL):
                    summed = summed + recv0[kind, g, j].astype(jnp.float32)
                tiles += [summed[k * SLAB:(k + 1) * SLAB] for k in range(MARGIN // W)]
            raws = [[blank, blank] + tiles[0:3], tiles[2:6] + [blank]]
            d = nt(
                jnp.concatenate(
                    [jnp.concatenate(r, axis=1) for r in raws], axis=0
                ).astype(jnp.bfloat16),
                ft,
            )
            wide = []
            for m in split_mag(d):
                m = m.astype(jnp.float32)
                left, right = m[0:SLAB], m[SLAB:]
                wide += [
                    jnp.concatenate(pair, axis=0)
                    for pair in ((blank, left), (left, right), (right, blank))
                ]
            d = divide(d, jnp.concatenate(wide, axis=1).astype(jnp.bfloat16))
            swap = jnp.concatenate([d[SLAB:], d[0:SLAB]], axis=0)

            @pl.when(l == LOCAL - 1)
            def _():
                old = part[g, 2 * SLAB * (per - 1):2 * SLAB * per].astype(jnp.float32)
                edge_row = (row >= SLAB) & (lane >= W - HALF_WIN)
                part[g, 2 * SLAB * (per - 1):2 * SLAB * per] = jnp.where(
                    edge_row, swap, old
                ).astype(jnp.bfloat16)

            @pl.when(l == 0)
            def _():
                old = part[g + 1, 0:2 * SLAB].astype(jnp.float32)
                edge_row = (row < SLAB) & (lane < HALF_WIN + TAPS // DECIM)
                part[g + 1, 0:2 * SLAB] = jnp.where(edge_row, swap, old).astype(jnp.bfloat16)

    each(Z - 1, lambda d: second(d + 1).start())
    for p in order[AHEAD[2]:AHEAD[3]]:
        all_bulk(p)

    pltpu.make_async_copy(recv2, recv2, r2_sem).wait()
    for g in range(T):
        summed = part[g].astype(jnp.float32)
        for j in range(Z - 1):
            summed = summed + recv2[j, g].astype(jnp.float32)
        mixed[g] = summed.astype(jnp.bfloat16)
    each(LOCAL - 1, lambda d: third(d + 1).start())
    pltpu.make_async_copy(mixed, recv3.at[l], r3_sem).start()
    @pl.when(t > 0)
    def _():
        to_right.wait_recv()

    @pl.when(t < T - 1)
    def _():
        to_left.wait_recv()

    decimate([0])
    past = nt(x_ref[:, 0:LEFT], ft[:, 3 * W:5 * W])
    keep = (t > 0) & (lax.broadcasted_iota(jnp.int32, (rows, W), 1) >= W - HALF_WIN)
    put_mag(-1, jnp.where(keep, past, 0.0))
    after = nt(x_ref[:, LEFT + raw_len - W:LEFT + raw_len + RIGHT], ft[:, 0:2 * W])
    keep = (t < T - 1) & (lax.broadcasted_iota(jnp.int32, (rows, W), 1) < HALF_WIN)
    put_mag(nb, jnp.where(keep, after, 0.0))
    whiten(edge)
    for p in order[AHEAD[3]:]:
        all_bulk(p)
    pltpu.make_async_copy(recv3, recv3, r3_sem).wait()

    gathered = jnp.concatenate(
        [
            recv3[p // per, g, p % per * 2 * SLAB:(p % per + 1) * 2 * SLAB]
            for g in range(T)
            for p in range(half)
        ],
        axis=1,
    )
    spread_row = lax.broadcasted_iota(jnp.int32, (2 * STEPS * SLAB, 2 * SLAB), 0)
    spread_col = lax.broadcasted_iota(jnp.int32, (2 * STEPS * SLAB, 2 * SLAB), 1)
    wanted = (spread_row // (STEPS * SLAB)) * SLAB + (spread_row // SLAB % STEPS) * step_len + (
        spread_row % step_len
    )
    spread = jnp.where(spread_col == wanted, 1.0, 0.0).astype(jnp.bfloat16)
    rep = jnp.dot(spread, gathered, preferred_element_type=jnp.float32)
    low = lax.broadcasted_iota(jnp.int32, (SLAB, W), 0) // step_len
    lane = lax.broadcasted_iota(jnp.int32, (SLAB, W), 1)
    zero = jnp.zeros((SLAB, W), jnp.float32)
    before = [zero] * STEPS
    turned = [[zero] * group] * STEPS
    line_ref[:, 0:W] = jnp.zeros((STEPS * SLAB, W), jnp.bfloat16)
    for q in range(T * nb + 1):
        plain = []
        for step in range(STEPS):
            if q < T * nb:
                top = (q % 2 * STEPS + step) * SLAB
                x = rep[top:top + SLAB, q // 2 * W:(q // 2 + 1) * W]
                turn = [x] + [pltpu.roll(x, k, 1) for k in range(1, group)]
            else:
                x, turn = zero, [zero] * group
            plain.append(x)
            for k in range(1, group):
                x = jnp.where(
                    low == k, jnp.where(lane >= k, turn[k], turned[step][k]), x
                )
            turned = turned[:step] + [turn] + turned[step + 1:]
            at = (q * STEPS + step) * SLAB
            window_ref[at:at + SLAB, 0:W] = before[step]
            window_ref[at:at + SLAB, W:] = x
            before[step] = x
        if q < T * nb - 1:
            line_ref[:, (q + 1) * W:(q + 2) * W] = jnp.concatenate(plain, axis=0).astype(
                jnp.bfloat16
            )
    batch = 12
    for q in range(0, T * nb + 1, batch):
        count = min(batch, T * nb + 1 - q)
        span = STEPS * SLAB
        moved = jnp.dot(
            window_ref[q * span:(q + count) * span, :].astype(jnp.bfloat16), shift_ref[...],
            preferred_element_type=jnp.float32,
        )
        for i in range(count):
            z = jnp.concatenate(
                [
                    moved[(i * STEPS + step) * SLAB:(i * STEPS + step + 1) * SLAB, v * W:(v + 1) * W]
                    for step in range(STEPS)
                    for v in range(tiles)
                ],
                axis=0,
            )
            shifted[(q + i + 1) * W:(q + i + 2) * W, :] = z.T.astype(jnp.bfloat16)

    groups = 2 * HALF_LAG // lags + 1

    def products(starts, count, fresh=False):
        w = jnp.concatenate([white_ref[:, pl.ds(aligned(n), count)] for n in starts], axis=1)
        for k in range(0, groups - 1, 2):
            b = jnp.concatenate(
                [
                    jnp.concatenate(
                        [
                            shifted[
                                pl.ds(pl.multiple_of(n + 2 * HALF_LAG - lags * m, 16), count), :
                            ]
                            for m in range(k, k + 2)
                        ],
                        axis=1,
                    )
                    for n in starts
                ],
                axis=0,
            )
            out = jnp.dot(w, b, preferred_element_type=jnp.float32)
            cols = slice(k * W, k * W + b.shape[1])
            if fresh:
                acc_ref[:, cols] = out
            else:
                acc_ref[:, cols] += out
        behind = jnp.concatenate([line_ref[:, pl.ds(aligned(n), count)] for n in starts], axis=1)
        if fresh:
            far_ref[...] = nt(behind, w)
        else:
            far_ref[...] += nt(behind, w)

    for q in range(0, dec_len, min(BLOCK, dec_len)):
        products([mine + q], min(BLOCK, dec_len), q == 0)

    def arrivals(d, _):
        begin = lax.rem(t + T - d, T) * dec_len
        for pairs in (order[:half - 2], edge):
            for i in pairs:
                cols = pl.ds(aligned(begin + i * 2 * W), 2 * W)
                pltpu.make_async_copy(
                    white_ref.at[:, cols], white_ref.at[:, cols], bulk_recv.at[d - 1, i]
                ).wait()
            if pairs[-1] - pairs[0] == len(pairs) - 1:
                products([begin + pairs[0] * 2 * W], len(pairs) * 2 * W)
            else:
                products([begin + i * 2 * W for i in pairs], 2 * W)
        return 0

    if T == 2:
        arrivals(1, 0)
    else:
        lax.fori_loop(1, T, arrivals, 0)

    for k in range(groups - 1):
        block = acc_ref[:, k * W:(k + 1) * W].T * scale
        for step in range(STEPS):
            to = (step * LAGS + k * lags) * step_len
            out_ref[to:to + tall, :] = block[step * tall:(step + 1) * tall, :]
    for step in range(STEPS):
        to = (step * LAGS + 2 * HALF_LAG) * step_len
        out_ref[to:to + step_len, :] = far_ref[step * SLAB:step * SLAB + step_len, :] * scale

    @pl.when(t < T - 1)
    def _():
        to_right.wait_send()

    @pl.when(t > 0)
    def _():
        to_left.wait_send()

    for which in outers:
        end_outer(*which)
    each(near - 1, lambda d: first(d + 1).wait_send())
    each(Z - 1, lambda d: second(d + 1).wait_send())
    each(LOCAL - 1, lambda d: third(d + 1).wait_send())
    for d in range(1, T):
        for i in range(half):
            bulk(d, i).wait_send()


def per_device(C, T, raw_strain, fir_taps, sources):
    rows, raw_len = raw_strain.shape
    dec_len = raw_len // DECIM
    nb = dec_len // W
    half = nb // 2
    tall = half // LOCAL * 2 * SLAB
    margin = (MARGIN // W + 1) * SLAB
    step_len = sources.shape[1] // T
    ns = STEPS * step_len
    total = T * dec_len
    groups = 2 * HALF_LAG // (W // ns) + 1
    bf, f32 = jnp.bfloat16, jnp.float32
    flat = pl.pallas_call(
        functools.partial(kernel, C, T, 1.0 / math.sqrt(total)),
        out_shape=pltpu.VMEM((STEPS * LAGS * step_len, rows), f32),
        in_specs=[
            pl.BlockSpec(memory_space=pltpu.HBM),
            pl.BlockSpec(memory_space=pltpu.HBM),
            pl.BlockSpec(memory_space=pltpu.HBM),
        ],
        out_specs=pl.BlockSpec(memory_space=pltpu.VMEM),
        scratch_shapes=[
            pltpu.VMEM((1, TAPS), bf),
            pltpu.SMEM(sources.shape, jnp.int32),
            pltpu.VMEM((T * SLAB, raw_len + (2 * DECIM + 1) * W), bf),
            pltpu.VMEM((rows, LEFT + raw_len + RIGHT), bf),
            pltpu.VMEM((rows, dec_len), f32),
            pltpu.VMEM((rows, dec_len + 2 * W), bf),
            pltpu.VMEM((rows, dec_len + 2 * W), bf),
            pltpu.VMEM((rows, total), bf),
            pltpu.VMEM((2, T, margin, W), bf),
            pltpu.VMEM((2, T - 1, LOCAL, margin, W), bf),
            pltpu.VMEM((LOCAL * T, tall, W), bf),
            pltpu.VMEM((LOCAL * T, tall, W), bf),
            pltpu.VMEM((T, tall, W), bf),
            pltpu.VMEM((C // LOCAL - 1, T, tall, W), bf),
            pltpu.VMEM((T, tall, W), bf),
            pltpu.VMEM((LOCAL, T, tall, W), bf),
            pltpu.VMEM(((T * nb + 1) * STEPS * SLAB, 2 * W), f32),
            pltpu.VMEM((2 * W, W // ns * step_len // SLAB * W), bf),
            pltpu.VMEM((total + 2 * W, W), bf),
            pltpu.VMEM((rows, groups * W - W), f32),
            pltpu.VMEM((STEPS * SLAB, total), bf),
            pltpu.VMEM((STEPS * SLAB, rows), f32),
            pltpu.SemaphoreType.DMA((2,)),
            pltpu.SemaphoreType.DMA((half,)),
            pltpu.SemaphoreType.DMA((2,)),
            pltpu.SemaphoreType.DMA((2,)),
            pltpu.SemaphoreType.DMA((2, 2, T)),
            pltpu.SemaphoreType.DMA,
            pltpu.SemaphoreType.DMA((LOCAL * T - 1,)),
            pltpu.SemaphoreType.DMA,
            pltpu.SemaphoreType.DMA((C // LOCAL - 1,)),
            pltpu.SemaphoreType.DMA,
            pltpu.SemaphoreType.DMA((LOCAL - 1,)),
            pltpu.SemaphoreType.DMA,
            pltpu.SemaphoreType.DMA((T, half)),
            pltpu.SemaphoreType.DMA((T, half)),
        ],
        compiler_params=pltpu.CompilerParams(
            collective_id=0, has_side_effects=True, vmem_limit_bytes=62 * 1024 * 1024
        ),
    )(raw_strain, fir_taps.reshape(1, TAPS), sources)
    return jnp.swapaxes(flat.reshape(STEPS, LAGS, step_len, rows), 1, 2)


def solution(mesh):
    C, T = mesh.shape["chan"], mesh.shape["tm"]
    return jax.shard_map(
        functools.partial(per_device, C, T),
        mesh=mesh,
        in_specs=(P("chan", "tm"), P(), P()),
        out_specs=P(None, "tm", None, "chan"),
        check_vma=False,
    )
```

```python
import functools
import math

import jax
import jax.numpy as jnp
from jax import lax
from jax.experimental import pallas as pl
from jax.experimental.pallas import tpu as pltpu
from jax.sharding import PartitionSpec as P

TAPS = 64
DECIM = 4
HALF_WIN = 32
LAGS = 257
HALF_LAG = 128
STEPS = 2
W = 128
SLAB = 8
LOCAL = 4
LEAD = 1
MARGIN = 384
PRE = 1
AHEAD = (1, 2, 4, 6)
BLOCK = 1024
LEFT = 256
RIGHT = 128
MESH = pl.DeviceIdType.MESH


def nt(a, b):
    return lax.dot_general(
        a, b, (((1,), (1,)), ((), ())), preferred_element_type=jnp.float32
    )


def aligned(x):
    return pl.multiple_of(x, W)


def kernel(
    C, T, scale,
    raw_ref, taps_hbm, src_hbm, out_ref,
    taps_ref, src_ref, praw_ref, x_ref, dec_ref, hi_ref, lo_ref, white_ref, send0, recv0, send1, recv1, part, recv2, mixed, recv3, window_ref, shift_ref, shifted, acc_ref, line_ref, far_ref,
    small_sem, load_sem, halo_send, halo_recv, s0_sem, r0_sem, s1_sem, r1_sem, s2_sem, r2_sem, s3_sem, r3_sem, bulk_send, bulk_recv,
):
    c = lax.axis_index("chan")
    t = lax.axis_index("tm")
    rows, raw_len = raw_ref.shape
    dec_len = raw_len // DECIM
    nb = dec_len // W
    half = nb // 2
    per = half // LOCAL
    step_len = src_hbm.shape[1] // T
    ns = STEPS * step_len
    total = T * dec_len
    mine = t * dec_len

    barrier = pltpu.get_barrier_semaphore()

    Z = C // LOCAL
    deck, l = c // LOCAL, lax.rem(c, LOCAL)
    near = LOCAL * T
    spot = l * T + t

    def beside(d):
        other = lax.rem(spot + d, near)
        return other // T, lax.rem(other, T)

    def along(d):
        return lax.rem(deck + d, Z) * LOCAL + l, t

    def greet_beside(d, _):
        to_l, to_t = beside(d)
        pl.semaphore_signal(
            barrier, inc=1, device_id=(deck * LOCAL + to_l, to_t), device_id_type=MESH
        )
        return 0

    def greet_along(d, _):
        pl.semaphore_signal(barrier, inc=1, device_id=along(d), device_id_type=MESH)
        return 0

    small = [
        pltpu.make_async_copy(taps_hbm, taps_ref, small_sem.at[0]),
        pltpu.make_async_copy(src_hbm, src_ref, small_sem.at[1]),
    ]
    for copy in small:
        copy.start()
    lax.fori_loop(1, Z, greet_along, 0)
    lax.fori_loop(1, near, greet_beside, 0)

    seg = raw_len // half
    loads = []
    for i in range(half):
        load = pltpu.make_async_copy(
            raw_ref.at[:, pl.ds(i * seg, seg)],
            x_ref.at[:, pl.ds(LEFT + i * seg, seg)],
            load_sem.at[i],
        )
        load.start()
        loads.append(load)

    to_right = pltpu.make_async_remote_copy(
        src_ref=raw_ref.at[:, pl.ds(raw_len - LEFT, LEFT)],
        dst_ref=x_ref.at[:, pl.ds(0, LEFT)],
        send_sem=halo_send.at[0], recv_sem=halo_recv.at[0],
        device_id=(c, lax.rem(t + 1, T)), device_id_type=MESH,
    )
    to_left = pltpu.make_async_remote_copy(
        src_ref=raw_ref.at[:, pl.ds(0, RIGHT)],
        dst_ref=x_ref.at[:, pl.ds(LEFT + raw_len, RIGHT)],
        send_sem=halo_send.at[1], recv_sem=halo_recv.at[1],
        device_id=(c, lax.rem(t + T - 1, T)), device_id_type=MESH,
    )

    @pl.when(t == 0)
    def _():
        x_ref[:, 0:LEFT] = jnp.zeros((rows, LEFT), jnp.bfloat16)

    @pl.when(t == T - 1)
    def _():
        x_ref[:, LEFT + raw_len:] = jnp.zeros((rows, RIGHT), jnp.bfloat16)

    span = lax.broadcasted_iota(jnp.int32, (2 * W, 4 * W), 1) - W - lax.broadcasted_iota(
        jnp.int32, (2 * W, 4 * W), 0
    )
    band = jnp.where((span >= -HALF_WIN) & (span <= HALF_WIN), 1.0, 0.0).astype(jnp.bfloat16)

    for copy in small:
        copy.wait()

    taps = jnp.broadcast_to(taps_ref[...], (16, TAPS))
    place = lax.broadcasted_iota(jnp.int32, (TAPS, W), 1) == lax.rem(
        W - lax.broadcasted_iota(jnp.int32, (TAPS, W), 0), W
    )
    base = jnp.dot(
        taps, place.astype(jnp.float32).astype(jnp.bfloat16), preferred_element_type=jnp.float32
    )
    rolled = pltpu.roll(
        jnp.broadcast_to(base[0:1, :], (W, W)), 0, 1, stride=DECIM, stride_axis=0
    )
    row_id = lax.broadcasted_iota(jnp.int32, (W, W), 0)
    lane_id = lax.broadcasted_iota(jnp.int32, (W, W), 1)
    fts = []
    for jc in range(DECIM + 1):
        k = DECIM * row_id + W - W * jc - lane_id
        fts.append(jnp.where((k >= 0) & (k < W), rolled, 0.0).astype(jnp.bfloat16))
    ft = jnp.concatenate(fts, axis=1)

    pr = lax.broadcasted_iota(jnp.int32, (T * SLAB, rows), 0)
    pc = lax.broadcasted_iota(jnp.int32, (T * SLAB, rows), 1)
    picks = jnp.zeros((T * SLAB, rows), jnp.float32)
    for g in range(T):
        for step in range(STEPS):
            for p in range(step_len):
                local = src_ref[step, g * step_len + p] - c * rows
                hit = (pr == g * SLAB + step * step_len + p) & (pc == local)
                picks = jnp.where(hit, 1.0, picks)
    picks = picks.astype(jnp.bfloat16)

    def put_mag(b, d):
        mag = jnp.abs(d)
        hi = mag.astype(jnp.bfloat16)
        hi_ref[:, (b + 1) * W:(b + 2) * W] = hi
        lo_ref[:, (b + 1) * W:(b + 2) * W] = (mag - hi.astype(jnp.float32)).astype(jnp.bfloat16)

    def decimate(blocks):
        begins = [LEFT - W + b * DECIM * W for b in blocks]
        x = jnp.concatenate([x_ref[:, a:a + (DECIM + 1) * W] for a in begins], axis=0)
        d = nt(x, ft)
        for i, b in enumerate(blocks):
            mine_d = d[i * rows:(i + 1) * rows]
            dec_ref[:, b * W:(b + 1) * W] = mine_d
            put_mag(b, mine_d)

    def first(d):
        to_l, g = beside(d)
        return pltpu.make_async_remote_copy(
            src_ref=send1.at[g * LOCAL + to_l], dst_ref=recv1.at[t * LOCAL + l],
            send_sem=s1_sem.at[d - 1], recv_sem=r1_sem,
            device_id=(deck * LOCAL + to_l, g), device_id_type=MESH,
        )

    def second(d):
        return pltpu.make_async_remote_copy(
            src_ref=part, dst_ref=recv2.at[d - 1],
            send_sem=s2_sem.at[d - 1], recv_sem=r2_sem,
            device_id=along(d), device_id_type=MESH,
        )

    def third(d):
        return pltpu.make_async_remote_copy(
            src_ref=mixed, dst_ref=recv3.at[l],
            send_sem=s3_sem.at[d - 1], recv_sem=r3_sem,
            device_id=(deck * LOCAL + lax.rem(l + d, LOCAL), t), device_id_type=MESH,
        )

    def bulk(d, i):
        cols = pl.ds(aligned(mine + i * 2 * W), 2 * W)
        return pltpu.make_async_remote_copy(
            src_ref=white_ref.at[:, cols], dst_ref=white_ref.at[:, cols],
            send_sem=bulk_send.at[d - 1, i], recv_sem=bulk_recv.at[d - 1, i],
            device_id=(c, lax.rem(t + d, T)), device_id_type=MESH,
        )

    def whiten(pairs):
        cols = [slice(2 * p * W, (2 * p + 4) * W) for p in pairs]
        sums = nt(jnp.concatenate([hi_ref[:, q] for q in cols], axis=0), band) + nt(
            jnp.concatenate([lo_ref[:, q] for q in cols], axis=0), band
        )
        level = sums / (2 * HALF_WIN + 1) + 1e-05
        for i, p in enumerate(pairs):
            d = dec_ref[:, 2 * p * W:2 * (p + 1) * W]
            w = (d / level[i * rows:(i + 1) * rows]).astype(jnp.bfloat16)
            white_ref[:, pl.ds(aligned(mine + 2 * p * W), 2 * W)] = w

    def all_bulk(i):
        for d in range(1, T):
            bulk(d, i).start()

    def each(count, body):
        if count <= 16:
            for i in range(count):
                body(i)
            return

        def step(i, _):
            body(i)
            return 0

        lax.fori_loop(0, count, step, 0)

    order = list(range(1, half - 1)) + [0, half - 1]
    lead = order[:LEAD]
    inner = order[LEAD:half - 2]
    edge = order[half - 2:]

    def pick_raw(x):
        return jnp.dot(picks, x, preferred_element_type=jnp.float32)

    def split_mag(d):
        mag = jnp.abs(d)
        hi = mag.astype(jnp.bfloat16)
        return hi, (mag - hi.astype(jnp.float32)).astype(jnp.bfloat16)

    narrow = band[0:W, 0:3 * W]
    narrow = jnp.concatenate([narrow, narrow], axis=1)

    def divide(d, wide):
        return d / (nt(wide, narrow) / (2 * HALF_WIN + 1) + 1e-05)

    split = 2 * LEAD + 3
    soon = -(-split // 2)
    for i in range(soon):
        loads[i].wait()
    decimate(range(1, split))
    whiten(lead)
    pl.semaphore_wait(barrier, near - 1 + Z - 1)

    for p in order[:PRE]:
        all_bulk(p)

    ahead = (DECIM + 1) * W
    many = T * SLAB
    praw_ref[:, 0:ahead] = jnp.zeros((many, ahead), jnp.bfloat16)
    for i in range(half):
        if i >= soon:
            loads[i].wait()
        x = pick_raw(x_ref[:, LEFT + i * seg:LEFT + (i + 1) * seg])
        praw_ref[:, ahead + i * seg:ahead + (i + 1) * seg] = x.astype(jnp.bfloat16)
        for kind, which, begin in ((0, half - 1, seg - MARGIN), (1, 0, 0)):
            if i == which:
                for g in range(T):
                    send0[kind, g] = jnp.concatenate(
                        [
                            x[g * SLAB:(g + 1) * SLAB, begin + k * W:begin + (k + 1) * W]
                            for k in range(MARGIN // W)
                        ]
                        + [jnp.zeros((SLAB, W), jnp.float32)],
                        axis=0,
                    ).astype(jnp.bfloat16)

    def outer(kind, e, g):
        to_l = e * (LOCAL - 1)
        slot = jnp.minimum(t, T - 2) if kind == 0 else jnp.maximum(t - 1, 0)
        inside = t < T - 1 if kind == 0 else t > 0
        same = (to_l == l) & (g == t)
        copy = pltpu.make_async_remote_copy(
            src_ref=send0.at[kind, g], dst_ref=recv0.at[kind, slot, l],
            send_sem=s0_sem.at[kind, e, g], recv_sem=r0_sem,
            device_id=(deck * LOCAL + to_l, g), device_id_type=MESH,
        )
        own = pltpu.make_async_copy(send0.at[kind, g], recv0.at[kind, slot, l], r0_sem)
        return inside & jnp.logical_not(same), inside & same, copy, own

    outers = [(kind, e, g) for kind in range(2) for e in range(2) for g in range(T)]

    def start_outer(kind, e, g):
        away, here, copy, own = outer(kind, e, g)

        @pl.when(away)
        def _():
            copy.start()

        @pl.when(here)
        def _():
            own.start()

    def end_outer(kind, e, g):
        away, here, copy, own = outer(kind, e, g)

        @pl.when(away)
        def _():
            copy.wait_send()

    for which in outers:
        start_outer(*which)

    d = nt(
        jnp.concatenate(
            [praw_ref[:, a:a + ahead] for a in [(b + 1) * DECIM * W for b in range(nb)]], axis=0
        ),
        ft,
    )
    none = jnp.zeros((many, W), jnp.bfloat16)
    mags = [jnp.concatenate([none, m, none], axis=0) for m in split_mag(d)]
    d = divide(
        d,
        jnp.concatenate(
            [m[k * many:(k + nb) * many] for m in mags for k in range(3)], axis=1
        ),
    )
    for p in range(half):
        at = p % per * 2 * SLAB
        for g in range(T):
            send1[g * LOCAL + p // per, at:at + 2 * SLAB] = jnp.concatenate(
                [
                    d[q * many + g * SLAB:q * many + (g + 1) * SLAB]
                    for q in (2 * p, 2 * p + 1)
                ],
                axis=0,
            ).astype(jnp.bfloat16)
    each(near - 1, lambda d: first(d + 1).start())
    pltpu.make_async_copy(
        send1.at[t * LOCAL + l], recv1.at[t * LOCAL + l], r1_sem
    ).start()
    @pl.when(t < T - 1)
    def _():
        to_right.start()

    @pl.when(t > 0)
    def _():
        to_left.start()

    for p in order[PRE:AHEAD[0]]:
        all_bulk(p)
    decimate(range(split, nb))
    whiten(inner)
    for p in order[AHEAD[0]:AHEAD[1]]:
        all_bulk(p)
    for p in order[AHEAD[1]:AHEAD[2]]:
        all_bulk(p)

    shifted[0:W, :] = jnp.zeros((W, W), jnp.bfloat16)
    lags = W // ns
    tall = lags * step_len
    tiles = tall // SLAB
    group = SLAB // step_len
    sample = lax.broadcasted_iota(jnp.int32, (2 * W, tiles * W), 0)
    place = lax.broadcasted_iota(jnp.int32, (2 * W, tiles * W), 1)
    shift = jnp.where(sample == W + place % W - place // W * group, 1.0, 0.0)
    shift_ref[...] = shift.astype(jnp.bfloat16)

    pltpu.make_async_copy(recv1, recv1, r1_sem).wait()
    for g in range(T):
        summed = recv1[g * LOCAL].astype(jnp.float32)
        for j in range(1, LOCAL):
            summed = summed + recv1[g * LOCAL + j].astype(jnp.float32)
        part[g] = summed.astype(jnp.bfloat16)

    @pl.when((l == 0) | (l == LOCAL - 1))
    def _():
        pltpu.make_async_copy(recv0, recv0, r0_sem).wait()
        row = lax.broadcasted_iota(jnp.int32, (2 * SLAB, W), 0)
        lane = lax.broadcasted_iota(jnp.int32, (2 * SLAB, W), 1)
        blank = jnp.zeros((SLAB, W), jnp.float32)
        for g in range(T - 1):
            tiles = []
            for kind in range(2):
                summed = recv0[kind, g, 0].astype(jnp.float32)
                for j in range(1, LOCAL):
                    summed = summed + recv0[kind, g, j].astype(jnp.float32)
                tiles += [summed[k * SLAB:(k + 1) * SLAB] for k in range(MARGIN // W)]
            raws = [[blank, blank] + tiles[0:3], tiles[2:6] + [blank]]
            d = nt(
                jnp.concatenate(
                    [jnp.concatenate(r, axis=1) for r in raws], axis=0
                ).astype(jnp.bfloat16),
                ft,
            )
            wide = []
            for m in split_mag(d):
                m = m.astype(jnp.float32)
                left, right = m[0:SLAB], m[SLAB:]
                wide += [
                    jnp.concatenate(pair, axis=0)
                    for pair in ((blank, left), (left, right), (right, blank))
                ]
            d = divide(d, jnp.concatenate(wide, axis=1).astype(jnp.bfloat16))
            swap = jnp.concatenate([d[SLAB:], d[0:SLAB]], axis=0)

            @pl.when(l == LOCAL - 1)
            def _():
                old = part[g, 2 * SLAB * (per - 1):2 * SLAB * per].astype(jnp.float32)
                edge_row = (row >= SLAB) & (lane >= W - HALF_WIN)
                part[g, 2 * SLAB * (per - 1):2 * SLAB * per] = jnp.where(
                    edge_row, swap, old
                ).astype(jnp.bfloat16)

            @pl.when(l == 0)
            def _():
                old = part[g + 1, 0:2 * SLAB].astype(jnp.float32)
                edge_row = (row < SLAB) & (lane < HALF_WIN + TAPS // DECIM)
                part[g + 1, 0:2 * SLAB] = jnp.where(edge_row, swap, old).astype(jnp.bfloat16)

    each(Z - 1, lambda d: second(d + 1).start())
    for p in order[AHEAD[2]:AHEAD[3]]:
        all_bulk(p)

    pltpu.make_async_copy(recv2, recv2, r2_sem).wait()
    for g in range(T):
        summed = part[g].astype(jnp.float32)
        for j in range(Z - 1):
            summed = summed + recv2[j, g].astype(jnp.float32)
        mixed[g] = summed.astype(jnp.bfloat16)
    each(LOCAL - 1, lambda d: third(d + 1).start())
    pltpu.make_async_copy(mixed, recv3.at[l], r3_sem).start()
    @pl.when(t > 0)
    def _():
        to_right.wait_recv()

    @pl.when(t < T - 1)
    def _():
        to_left.wait_recv()

    decimate([0])
    past = nt(x_ref[:, 0:LEFT], ft[:, 3 * W:5 * W])
    keep = (t > 0) & (lax.broadcasted_iota(jnp.int32, (rows, W), 1) >= W - HALF_WIN)
    put_mag(-1, jnp.where(keep, past, 0.0))
    after = nt(x_ref[:, LEFT + raw_len - W:LEFT + raw_len + RIGHT], ft[:, 0:2 * W])
    keep = (t < T - 1) & (lax.broadcasted_iota(jnp.int32, (rows, W), 1) < HALF_WIN)
    put_mag(nb, jnp.where(keep, after, 0.0))
    whiten(edge)
    for p in order[AHEAD[3]:]:
        all_bulk(p)
    pltpu.make_async_copy(recv3, recv3, r3_sem).wait()

    gathered = jnp.concatenate(
        [
            recv3[p // per, g, p % per * 2 * SLAB:(p % per + 1) * 2 * SLAB]
            for g in range(T)
            for p in range(half)
        ],
        axis=1,
    )
    spread_row = lax.broadcasted_iota(jnp.int32, (2 * STEPS * SLAB, 2 * SLAB), 0)
    spread_col = lax.broadcasted_iota(jnp.int32, (2 * STEPS * SLAB, 2 * SLAB), 1)
    wanted = (spread_row // (STEPS * SLAB)) * SLAB + (spread_row // SLAB % STEPS) * step_len + (
        spread_row % step_len
    )
    spread = jnp.where(spread_col == wanted, 1.0, 0.0).astype(jnp.bfloat16)
    rep = jnp.dot(spread, gathered, preferred_element_type=jnp.float32)
    low = lax.broadcasted_iota(jnp.int32, (SLAB, W), 0) // step_len
    lane = lax.broadcasted_iota(jnp.int32, (SLAB, W), 1)
    zero = jnp.zeros((SLAB, W), jnp.float32)
    before = [zero] * STEPS
    turned = [[zero] * group] * STEPS
    line_ref[:, 0:W] = jnp.zeros((STEPS * SLAB, W), jnp.bfloat16)
    for q in range(T * nb + 1):
        plain = []
        for step in range(STEPS):
            if q < T * nb:
                top = (q % 2 * STEPS + step) * SLAB
                x = rep[top:top + SLAB, q // 2 * W:(q // 2 + 1) * W]
                turn = [x] + [pltpu.roll(x, k, 1) for k in range(1, group)]
            else:
                x, turn = zero, [zero] * group
            plain.append(x)
            for k in range(1, group):
                x = jnp.where(
                    low == k, jnp.where(lane >= k, turn[k], turned[step][k]), x
                )
            turned = turned[:step] + [turn] + turned[step + 1:]
            at = (q * STEPS + step) * SLAB
            window_ref[at:at + SLAB, 0:W] = before[step]
            window_ref[at:at + SLAB, W:] = x
            before[step] = x
        if q < T * nb - 1:
            line_ref[:, (q + 1) * W:(q + 2) * W] = jnp.concatenate(plain, axis=0).astype(
                jnp.bfloat16
            )
    batch = 12
    for q in range(0, T * nb + 1, batch):
        count = min(batch, T * nb + 1 - q)
        span = STEPS * SLAB
        moved = jnp.dot(
            window_ref[q * span:(q + count) * span, :].astype(jnp.bfloat16), shift_ref[...],
            preferred_element_type=jnp.float32,
        )
        for i in range(count):
            z = jnp.concatenate(
                [
                    moved[(i * STEPS + step) * SLAB:(i * STEPS + step + 1) * SLAB, v * W:(v + 1) * W]
                    for step in range(STEPS)
                    for v in range(tiles)
                ],
                axis=0,
            )
            shifted[(q + i + 1) * W:(q + i + 2) * W, :] = z.T.astype(jnp.bfloat16)

    groups = 2 * HALF_LAG // lags + 1

    def products(starts, count, fresh=False):
        w = jnp.concatenate([white_ref[:, pl.ds(aligned(n), count)] for n in starts], axis=1)
        for k in range(0, groups - 1, 2):
            b = jnp.concatenate(
                [
                    jnp.concatenate(
                        [
                            shifted[
                                pl.ds(pl.multiple_of(n + 2 * HALF_LAG - lags * m, 16), count), :
                            ]
                            for m in range(k, k + 2)
                        ],
                        axis=1,
                    )
                    for n in starts
                ],
                axis=0,
            )
            out = jnp.dot(w, b, preferred_element_type=jnp.float32)
            cols = slice(k * W, k * W + b.shape[1])
            if fresh:
                acc_ref[:, cols] = out
            else:
                acc_ref[:, cols] += out
        behind = jnp.concatenate([line_ref[:, pl.ds(aligned(n), count)] for n in starts], axis=1)
        if fresh:
            far_ref[...] = nt(behind, w)
        else:
            far_ref[...] += nt(behind, w)

    for q in range(0, dec_len, min(BLOCK, dec_len)):
        products([mine + q], min(BLOCK, dec_len), q == 0)

    def arrivals(d, _):
        begin = lax.rem(t + T - d, T) * dec_len
        for pairs in (order[:half - 2], edge):
            for i in pairs:
                cols = pl.ds(aligned(begin + i * 2 * W), 2 * W)
                pltpu.make_async_copy(
                    white_ref.at[:, cols], white_ref.at[:, cols], bulk_recv.at[d - 1, i]
                ).wait()
            if pairs[-1] - pairs[0] == len(pairs) - 1:
                products([begin + pairs[0] * 2 * W], len(pairs) * 2 * W)
            else:
                products([begin + i * 2 * W for i in pairs], 2 * W)
        return 0

    if T == 2:
        arrivals(1, 0)
    else:
        lax.fori_loop(1, T, arrivals, 0)

    for k in range(groups - 1):
        block = acc_ref[:, k * W:(k + 1) * W].T * scale
        for step in range(STEPS):
            to = (step * LAGS + k * lags) * step_len
            out_ref[to:to + tall, :] = block[step * tall:(step + 1) * tall, :]
    for step in range(STEPS):
        to = (step * LAGS + 2 * HALF_LAG) * step_len
        out_ref[to:to + step_len, :] = far_ref[step * SLAB:step * SLAB + step_len, :] * scale

    @pl.when(t < T - 1)
    def _():
        to_right.wait_send()

    @pl.when(t > 0)
    def _():
        to_left.wait_send()

    for which in outers:
        end_outer(*which)
    each(near - 1, lambda d: first(d + 1).wait_send())
    each(Z - 1, lambda d: second(d + 1).wait_send())
    each(LOCAL - 1, lambda d: third(d + 1).wait_send())
    for d in range(1, T):
        for i in range(half):
            bulk(d, i).wait_send()


def per_device(C, T, raw_strain, fir_taps, sources):
    rows, raw_len = raw_strain.shape
    dec_len = raw_len // DECIM
    nb = dec_len // W
    half = nb // 2
    tall = half // LOCAL * 2 * SLAB
    margin = (MARGIN // W + 1) * SLAB
    step_len = sources.shape[1] // T
    ns = STEPS * step_len
    total = T * dec_len
    groups = 2 * HALF_LAG // (W // ns) + 1
    bf, f32 = jnp.bfloat16, jnp.float32
    flat = pl.pallas_call(
        functools.partial(kernel, C, T, 1.0 / math.sqrt(total)),
        out_shape=pltpu.VMEM((STEPS * LAGS * step_len, rows), f32),
        in_specs=[
            pl.BlockSpec(memory_space=pltpu.HBM),
            pl.BlockSpec(memory_space=pltpu.HBM),
            pl.BlockSpec(memory_space=pltpu.HBM),
        ],
        out_specs=pl.BlockSpec(memory_space=pltpu.VMEM),
        scratch_shapes=[
            pltpu.VMEM((1, TAPS), bf),
            pltpu.SMEM(sources.shape, jnp.int32),
            pltpu.VMEM((T * SLAB, raw_len + (2 * DECIM + 1) * W), bf),
            pltpu.VMEM((rows, LEFT + raw_len + RIGHT), bf),
            pltpu.VMEM((rows, dec_len), f32),
            pltpu.VMEM((rows, dec_len + 2 * W), bf),
            pltpu.VMEM((rows, dec_len + 2 * W), bf),
            pltpu.VMEM((rows, total), bf),
            pltpu.VMEM((2, T, margin, W), bf),
            pltpu.VMEM((2, T - 1, LOCAL, margin, W), bf),
            pltpu.VMEM((LOCAL * T, tall, W), bf),
            pltpu.VMEM((LOCAL * T, tall, W), bf),
            pltpu.VMEM((T, tall, W), bf),
            pltpu.VMEM((C // LOCAL - 1, T, tall, W), bf),
            pltpu.VMEM((T, tall, W), bf),
            pltpu.VMEM((LOCAL, T, tall, W), bf),
            pltpu.VMEM(((T * nb + 1) * STEPS * SLAB, 2 * W), f32),
            pltpu.VMEM((2 * W, W // ns * step_len // SLAB * W), bf),
            pltpu.VMEM((total + 2 * W, W), bf),
            pltpu.VMEM((rows, groups * W - W), f32),
            pltpu.VMEM((STEPS * SLAB, total), bf),
            pltpu.VMEM((STEPS * SLAB, rows), f32),
            pltpu.SemaphoreType.DMA((2,)),
            pltpu.SemaphoreType.DMA((half,)),
            pltpu.SemaphoreType.DMA((2,)),
            pltpu.SemaphoreType.DMA((2,)),
            pltpu.SemaphoreType.DMA((2, 2, T)),
            pltpu.SemaphoreType.DMA,
            pltpu.SemaphoreType.DMA((LOCAL * T - 1,)),
            pltpu.SemaphoreType.DMA,
            pltpu.SemaphoreType.DMA((C // LOCAL - 1,)),
            pltpu.SemaphoreType.DMA,
            pltpu.SemaphoreType.DMA((LOCAL - 1,)),
            pltpu.SemaphoreType.DMA,
            pltpu.SemaphoreType.DMA((T, half)),
            pltpu.SemaphoreType.DMA((T, half)),
        ],
        compiler_params=pltpu.CompilerParams(
            collective_id=0, has_side_effects=True, vmem_limit_bytes=62 * 1024 * 1024
        ),
    )(raw_strain, fir_taps.reshape(1, TAPS), sources)
    return jnp.swapaxes(flat.reshape(STEPS, LAGS, step_len, rows), 1, 2)


def solution(mesh):
    C, T = mesh.shape["chan"], mesh.shape["tm"]
    return jax.shard_map(
        functools.partial(per_device, C, T),
        mesh=mesh,
        in_specs=(P("chan", "tm"), P(), P()),
        out_specs=P(None, "tm", None, "chan"),
        check_vma=False,
    )
```
